512 devices in a mesh: tm: 8 (over y), bl: 32 (over x, z_lo, core), chan: 2 (over z_hi).
Axes of the slice: x: 4, y: 8, z: 8 (z_hi: 2, z_lo: 4; z = z_hi * 4 + z_lo), core: 2. Of those that a mesh axis runs over, the one named last changes fastest.
Arguments:
- model: bfloat16 [8, 4, 8, 8, 8192], P('tm', 'chan', None, None, 'bl'), may hold values from -2.5 to 2.5
- vis: float32 [8, 4, 8, 8192], P('tm', 'chan', None, 'bl'), may hold values from -6 to 6
- weights: float32 [8, 4, 8192], P('tm', 'chan', 'bl'), may hold values from 0.2 to 4
- antenna1: int32 [8192], P('bl'), may hold values from 0 to 511, as said below
- antenna2: int32 [8192], P('bl'), may hold values from 0 to 511
- live: int32 [8192], P('bl'), may hold values from 0 to 1, as said below
- gains: float32 [2, 8, 8, 512], P('chan', None, None, 'bl'), may hold values from -3 to 3
Outputs:
- gains_out: float32 [2, 8, 8, 512], P('chan', None, None, 'bl')
- whitened: float32 [2, 8, 8, 512], P('chan', None, None, 'bl')
The draws below stay inside these ranges and needn't reach their ends.
Inputs may be any that keep to these rules, and one draw needn't show every extreme that they name: antenna1 and antenna2 differ on every baseline. `live`: padded slots are marked 0.
All inputs are finite; a program needn't handle non-finite values.
Results may differ from the reference program's by a relative error of at most 0.0003.
Values sent between devices are 32-bit elements; how exact they have to be, the bound alone decides.
No kernel may reach another device: no remote copies, remote signals or barrier semaphores. Data moves between devices by JAX's collectives and lax.ppermute only.
A program may use at most 64 MiB of HBM per device.

```python
import math
import jax
import jax.numpy as jnp
from jax import lax

S = 512
K = 8
CH_DEV = 2
ITERS = 3
NT = 8
NCB = 2
NCH = 4
NB = 8192
N_CHAN = 2


def pair_tables(key):
    slots = S * S // 2
    order = jax.random.permutation(key, max(NB, slots))
    slot = (order[:NB] % slots).astype(jnp.int32)
    station = slot % S
    offset = slot // S + 1
    other = (station + offset) % S
    usable = jnp.where((offset == S // 2) & (station >= S // 2), 0, 1).astype(jnp.int32)
    return (station.astype(jnp.int32), other.astype(jnp.int32), usable)


def draw_antenna1(key, part):
    return pair_tables(key)[0]


def draw_antenna2(key, part):
    return pair_tables(key)[1]


def draw_live(key, part):
    return pair_tables(key)[2]


def block_scale(key, extent, pieces, smallest, high):
    factor_of = 1.0
    for axis_at, blocks in pieces:
        draws = jax.random.uniform(jax.random.fold_in(jax.random.fold_in(key, 6), axis_at), (blocks,), jnp.float32, smallest / len(pieces), high / len(pieces))
        factor_of = factor_of * jnp.repeat(jnp.exp(draws), extent[axis_at] // blocks).reshape((-1,) + (1,) * (len(extent) - 1 - axis_at))
    return factor_of


def bell_draw(stream_key, shape, spread, bound, cuts=(), kind=jnp.bfloat16):
    entries = spread * jax.random.normal(stream_key, shape, jnp.float32)
    if cuts:
        entries = entries * block_scale(stream_key, shape, cuts, -0.22, 0.18)
    return jnp.clip(entries, -bound, bound).astype(kind)


def setup_inputs(seed: int = 0) -> dict:
    key_of = jax.random.split(jax.random.key(seed), 8)
    model = bell_draw(key_of[0], (NT, NCH, K, 8, NB), 0.35, 2.5, ((0, 8), (1, 2), (4, 32)))
    vis = bell_draw(key_of[1], (NT, NCH, 8, NB), 1.0, 6.0, ((0, 8), (1, 2), (3, 32)), jnp.float32)
    weights = jnp.clip(jnp.exp(math.log(4.0) - 2.9957323 * jax.random.uniform(key_of[2], (NT, NCH, NB), jnp.float32) ** block_scale(key_of[2], (NT, NCH, NB), ((0, 8), (1, 2), (2, 32)), -0.2, 0.2)), 0.2, 4.0)
    antenna1 = draw_antenna1(jax.random.fold_in(key_of[7], 71), 0)
    antenna2 = draw_antenna2(jax.random.fold_in(key_of[7], 71), 0)
    live = draw_live(jax.random.fold_in(key_of[7], 71), 0)
    gains = bell_draw(key_of[6], (NCB, K, 8, S), 0.5, 3.0, ((0, 2), (3, 32)), jnp.float32)
    return {"model": model, "vis": vis, "weights": weights, "antenna1": antenna1, "antenna2": antenna2, "live": live, "gains": gains}


step_scale = 0.8

def jones(array):
    return [(array[..., index, :], array[..., index + 4, :]) for index in range(4)]

def cmul(left, right):
    return (left[0] * right[0] - left[1] * right[1], left[0] * right[1] + left[1] * right[0])

def cadd(left, right):
    return (left[0] + right[0], left[1] + right[1])

def adjoint(matrix):
    return [(entry[0], -entry[1]) for entry in (matrix[0], matrix[2], matrix[1], matrix[3])]

def product(left, right):
    result = []
    for row in range(2):
        for col in range(2):
            result.append(cadd(cmul(left[2 * row], right[col]), cmul(left[2 * row + 1], right[2 + col])))
    return result

def stack_jones(matrix):
    return jnp.stack([entry[0] for entry in matrix] + [entry[1] for entry in matrix], axis=-2)

def norm_sq(matrix):
    return sum((entry[0] * entry[0] + entry[1] * entry[1] for entry in matrix))

def baseline_terms(near, far, model, vis, weight):
    near_j = jones(near)
    far_j = jones(far)
    model_j = jones(model)
    right_a = product(model_j, adjoint(far_j))
    left_b = product(near_j, model_j)
    each = product(near_j, right_a)
    observed = jones(vis[..., None, :, :])
    scale = weight[..., None, :]
    resid = []
    for index in range(4):
        pred_re = lax.optimization_barrier(jnp.sum(each[index][0], axis=-2, keepdims=True))
        pred_im = lax.optimization_barrier(jnp.sum(each[index][1], axis=-2, keepdims=True))
        resid.append((scale * (observed[index][0] - pred_re), scale * (observed[index][1] - pred_im)))
    term_p = -stack_jones(product(resid, adjoint(right_a)))
    term_q = -stack_jones(product(adjoint(resid), left_b))
    curv_p = scale * norm_sq(right_a)
    curv_q = scale * norm_sq(left_b)
    return (term_p, term_q, curv_p, curv_q)

def reference(model, vis, weights, antenna1, antenna2, live, gains):
    live_f = live.astype(jnp.float32)
    outs_gain = []
    outs_white = []
    for block in range(N_CHAN):
        current = gains[block]
        white = jnp.zeros_like(current)
        for step in range(ITERS):
            near = jnp.take(current, antenna1, axis=2)
            far = jnp.take(current, antenna2, axis=2)

            def slab(carry, index):
                tidx = index // CH_DEV
                cidx = block * CH_DEV + index % CH_DEV
                mdl = model[tidx, cidx].astype(jnp.float32)
                terms = baseline_terms(near, far, mdl, vis[tidx, cidx], weights[tidx, cidx] * live_f)
                return (tuple((a + b for a, b in zip(carry, terms))), None)
            zero_big = jnp.zeros((K, 8, NB), jnp.float32)
            zero_small = jnp.zeros((K, NB), jnp.float32)
            (term_p, term_q, curv_p, curv_q), _ = lax.scan(slab, (zero_big, zero_big, zero_small, zero_small), jnp.arange(NT * CH_DEV, dtype=jnp.int32))
            flat_p = jnp.concatenate([term_p.reshape(K * 8, NB), curv_p], axis=0)
            flat_q = jnp.concatenate([term_q.reshape(K * 8, NB), curv_q], axis=0)
            station = (jax.ops.segment_sum(flat_p.T, antenna1, num_segments=S) + jax.ops.segment_sum(flat_q.T, antenna2, num_segments=S)).T
            grad = station[:K * 8].reshape(K, 8, S)
            denom = station[K * 8:][:, None, :] + 1.0
            white = grad / jnp.sqrt(denom)
            current = current - step_scale * grad / denom
        outs_gain.append(current)
        outs_white.append(white)
    return (jnp.stack(outs_gain), jnp.stack(outs_white))
```

```python
import functools

import jax
import jax.numpy as jnp
from jax import lax
from jax.experimental import pallas as pl
from jax.experimental.pallas import tpu as pltpu
from jax.sharding import Mesh
from jax.sharding import PartitionSpec as P

ITERS = 3
STEP = 0.8
DIRS = 8
COMPS = 8
VALS = DIRS * COMPS
LANES = 128
RUN = LANES // DIRS


def cmul(left, right):
    return (left[0] * right[0] - left[1] * right[1], left[0] * right[1] + left[1] * right[0])


def cadd(left, right):
    return (left[0] + right[0], left[1] + right[1])


def adjoint(matrix):
    return [(entry[0], -entry[1]) for entry in (matrix[0], matrix[2], matrix[1], matrix[3])]


def product(left, right):
    result = []
    for row in range(2):
        for col in range(2):
            result.append(
                cadd(cmul(left[2 * row], right[col]), cmul(left[2 * row + 1], right[2 + col]))
            )
    return result


def norm_sq(matrix):
    return sum(entry[0] * entry[0] + entry[1] * entry[1] for entry in matrix)


def halves(value):
    high = value.astype(jnp.bfloat16)
    low = (value - high.astype(jnp.float32)).astype(jnp.bfloat16)
    return high, low


def select_sum(left, right, dims):
    total = None
    for part in halves(left):
        term = lax.dot_general(
            part, right, (dims, ((), ())), preferred_element_type=jnp.float32
        )
        total = term if total is None else total + term
    return total


def pick_sum(left, right, dims):
    total = None
    for part in halves(right):
        term = lax.dot_general(
            left, part, (dims, ((), ())), preferred_element_type=jnp.float32
        )
        total = term if total is None else total + term
    return total


def partials_kernel(
    gains_ref, model_ref, vis_ref, weight_ref, live_ref, first_ref, second_ref,
    out_ref, picked_ref, model_f_ref, terms_ref,
):
    base = first_ref.shape[1]
    pairs = gains_ref.shape[0]
    channels = model_ref.shape[0]
    station = jnp.concatenate([first_ref[...], second_ref[...]], axis=1)
    rows = lax.broadcasted_iota(jnp.int32, (pairs, 2 * base), 0)
    hot = jnp.where(rows == station // 2, 1.0, 0.0).astype(jnp.bfloat16)
    odd = station % 2 == 1

    both = select_sum(gains_ref[...].T, hot, ((1,), (0,)))
    picked = jnp.where(odd, both[VALS:], both[:VALS])
    cuts = base // LANES
    for cut in range(2 * cuts):
        picked_ref[cut] = picked[:, cut * LANES : (cut + 1) * LANES]

    def entries(ref, at):
        comps = [ref[at, pl.ds(c, DIRS, stride=COMPS), :] for c in range(COMPS)]
        return [(comps[i], comps[i + 4]) for i in range(4)]

    live = live_ref[...].astype(jnp.float32)
    curvs = [None] * (2 * cuts)
    for cut in range(cuts):
        lanes = slice(cut * LANES, (cut + 1) * LANES)
        near = entries(picked_ref, cut)
        far = entries(picked_ref, cuts + cut)
        totals = None
        for channel in range(channels):
            model_f_ref[0] = model_ref[channel, :, lanes].astype(jnp.float32)
            model = entries(model_f_ref, 0)
            scale = weight_ref[channel : channel + 1, lanes] * live[:, lanes]
            right_a = product(model, adjoint(far))
            left_b = product(near, model)
            each = product(near, right_a)
            vis = vis_ref[channel, :, lanes]
            resid = []
            for index in range(4):
                pred_re = jnp.sum(each[index][0], axis=0, keepdims=True)
                pred_im = jnp.sum(each[index][1], axis=0, keepdims=True)
                resid.append(
                    (
                        scale * (vis[index : index + 1] - pred_re),
                        scale * (vis[index + 4 : index + 5] - pred_im),
                    )
                )
            new = (
                product(resid, adjoint(right_a)),
                product(adjoint(resid), left_b),
                scale * norm_sq(right_a),
                scale * norm_sq(left_b),
            )
            totals = new if totals is None else jax.tree.map(lambda a, b: a + b, totals, new)
        for side in range(2):
            at = side * cuts + cut
            for index, (real, imag) in enumerate(totals[side]):
                terms_ref[at, pl.ds(index, DIRS, stride=COMPS), :] = -real
                terms_ref[at, pl.ds(index + 4, DIRS, stride=COMPS), :] = -imag
            curvs[at] = totals[2 + side]

    terms = jnp.concatenate([terms_ref[at] for at in range(2 * cuts)], axis=1)
    curv = jnp.concatenate(curvs, axis=1)
    spread = jnp.concatenate([jnp.where(odd, 0.0, terms), jnp.where(odd, terms, 0.0)], axis=0)
    grads = pick_sum(hot, spread, ((1,), (1,)))
    place = station % RUN
    spread = jnp.concatenate([jnp.where(place == j, curv, 0.0) for j in range(RUN)], axis=0)
    rows = lax.broadcasted_iota(jnp.int32, (2 * pairs // RUN, 2 * base), 0)
    hot = jnp.where(rows == station // RUN, 1.0, 0.0).astype(jnp.bfloat16)
    curvs = pick_sum(hot, spread, ((1,), (1,)))
    for peer in range(pairs // RUN):
        at = peer * (RUN + 2)
        out_ref[at : at + RUN, :] = grads[peer * RUN : (peer + 1) * RUN]
        out_ref[at + RUN : at + RUN + 2, :] = curvs[2 * peer : 2 * peer + 2]


def partials(gains, model, vis, weights, live, first, second):
    pairs = gains.shape[0]
    base = first.shape[1]
    return pl.pallas_call(
        partials_kernel,
        out_shape=jax.ShapeDtypeStruct((pairs // RUN * (RUN + 2), LANES), jnp.float32),
        in_specs=[pl.BlockSpec(memory_space=pltpu.VMEM)] * 7,
        out_specs=pl.BlockSpec(memory_space=pltpu.VMEM),
        scratch_shapes=[
            pltpu.VMEM((2 * base // LANES, VALS, LANES), jnp.float32),
            pltpu.VMEM((1, VALS, LANES), jnp.float32),
            pltpu.VMEM((2 * base // LANES, VALS, LANES), jnp.float32),
        ],
        compiler_params=pltpu.CompilerParams(vmem_limit_bytes=16 * 2**20),
        name="partials",
    )(gains, model, vis, weights, live, first, second)


def peers_sum(parts_ref, rows):
    total = parts_ref[0:rows, :]
    for at in range(rows, parts_ref.shape[0], rows):
        total = total + parts_ref[at : at + rows, :]
    return total


def total_kernel(parts_ref, copies_ref):
    rows = RUN + 2
    total = peers_sum(parts_ref, rows)
    for at in range(0, copies_ref.shape[0], rows):
        copies_ref[at : at + rows, :] = total


def total(parts, peers):
    return pl.pallas_call(
        total_kernel,
        out_shape=jax.ShapeDtypeStruct((peers * (RUN + 2), LANES), jnp.float32),
        in_specs=[pl.BlockSpec(memory_space=pltpu.VMEM)],
        out_specs=pl.BlockSpec(memory_space=pltpu.VMEM),
        compiler_params=pltpu.CompilerParams(vmem_limit_bytes=16 * 2**20),
        name="total",
    )(parts)


def stepped(at_ref, parts_ref, gains_ref):
    sums = peers_sum(parts_ref, RUN + 2)
    grad = sums[:RUN]
    row = lax.broadcasted_iota(jnp.int32, (RUN, LANES), 0)
    lane = lax.broadcasted_iota(jnp.int32, (RUN, LANES), 1)
    curv = jnp.where(row < RUN // 2, sums[RUN : RUN + 1], sums[RUN + 1 : RUN + 2])
    curv = jnp.where(lane // (2 * DIRS) == row % (RUN // 2), curv, 0.0)
    source = lax.broadcasted_iota(jnp.int32, (LANES, LANES), 0)
    target = lax.broadcasted_iota(jnp.int32, (LANES, LANES), 1)
    wide = jnp.where(source % (2 * DIRS) == target // COMPS, 1.0, 0.0)
    denom = 1.0 + jnp.dot(
        curv, wide, precision=lax.Precision.HIGHEST, preferred_element_type=jnp.float32
    )
    old = gains_ref[pl.ds(pl.multiple_of(at_ref[0], RUN), RUN), :]
    return old - STEP * grad / denom, grad / jnp.sqrt(denom)


def step_kernel(at_ref, parts_ref, gains_ref, copies_ref):
    gains, _ = stepped(at_ref, parts_ref, gains_ref)
    for at in range(0, copies_ref.shape[0], RUN):
        copies_ref[at : at + RUN, :] = gains


def last_kernel(at_ref, parts_ref, gains_ref, gains_out_ref, white_ref, rows_ref):
    half = RUN // 2
    source = lax.broadcasted_iota(jnp.int32, (half, RUN), 0)
    target = lax.broadcasted_iota(jnp.int32, (half, RUN), 1)
    for value, out_ref in zip(stepped(at_ref, parts_ref, gains_ref), (gains_out_ref, white_ref)):
        rows_ref[...] = value
        turned = rows_ref[pl.ds(pl.multiple_of(at_ref[1], half), half), :].T
        out = None
        for odd in range(2):
            place = jnp.where(target == 2 * source + odd, 1.0, 0.0)
            part = jnp.dot(
                turned[odd * VALS : (odd + 1) * VALS],
                place,
                precision=lax.Precision.HIGHEST,
                preferred_element_type=jnp.float32,
            )
            out = part if out is None else out + part
        out_ref[...] = out


def step(at, parts, gains, peers):
    return pl.pallas_call(
        step_kernel,
        out_shape=jax.ShapeDtypeStruct((peers * RUN, LANES), jnp.float32),
        in_specs=[pl.BlockSpec(memory_space=pltpu.SMEM)]
        + [pl.BlockSpec(memory_space=pltpu.VMEM)] * 2,
        out_specs=pl.BlockSpec(memory_space=pltpu.VMEM),
        compiler_params=pltpu.CompilerParams(vmem_limit_bytes=16 * 2**20),
        name="step",
    )(at, parts, gains)


def last(at, parts, gains):
    return pl.pallas_call(
        last_kernel,
        out_shape=(jax.ShapeDtypeStruct((VALS, RUN), jnp.float32),) * 2,
        in_specs=[pl.BlockSpec(memory_space=pltpu.SMEM)]
        + [pl.BlockSpec(memory_space=pltpu.VMEM)] * 2,
        out_specs=(pl.BlockSpec(memory_space=pltpu.VMEM),) * 2,
        scratch_shapes=[pltpu.VMEM((RUN, LANES), jnp.float32)],
        compiler_params=pltpu.CompilerParams(vmem_limit_bytes=16 * 2**20),
        name="last",
    )(at, parts, gains)


def exchange(rows, axes, peers):
    count = rows.shape[0]
    sent = rows.reshape(peers, 1, count // peers * LANES)
    return lax.all_to_all(sent, axes, 0, 0).reshape(count, LANES)


def per_device(model, vis, weights, antenna1, antenna2, live, gains):
    base = antenna1.shape[0]
    channels = model.shape[1]
    owned = gains.shape[3]
    chips, others = ("x", "z"), ("y", "core")
    model = model.reshape(channels, VALS, base)
    vis, weights = vis[0], weights[0]
    first, second, live = (a.reshape(1, base) for a in (antenna1, antenna2, live))
    mine = gains.reshape(VALS, owned).T.reshape(1, owned * VALS // LANES, LANES)
    mine = jnp.broadcast_to(mine, (32,) + mine.shape[1:]).reshape(-1, LANES)
    full = exchange(mine, ("x", "z", "core"), 32)
    chip = lax.axis_index("x") * 4 + lax.axis_index("z")
    at = jnp.stack([chip * RUN, lax.axis_index("core") * (RUN // 2)]).astype(jnp.int32)
    for turn in range(ITERS):
        sent = partials(full, model, vis, weights, live, first, second)
        sent = total(exchange(sent, chips, 16), 16)
        sums = exchange(sent, others, 16)
        if turn < ITERS - 1:
            full = exchange(step(at, sums, full, 16), chips, 16)
    return tuple(out.reshape(gains.shape) for out in last(at, sums, full))


def solution(mesh):
    fine = Mesh(mesh.devices.reshape(8, 4, 4, 2, 2), ("y", "x", "z", "core", "chan"))
    bl = ("x", "z", "core")
    return jax.shard_map(
        per_device,
        mesh=fine,
        in_specs=(
            P("y", "chan", None, None, bl),
            P("y", "chan", None, bl),
            P("y", "chan", bl),
            P(bl),
            P(bl),
            P(bl),
            P("chan", None, None, bl),
        ),
        out_specs=(P("chan", None, None, bl), P("chan", None, None, bl)),
        check_vma=False,
    )
```

```python
import functools

import jax
import jax.numpy as jnp
from jax import lax
from jax.experimental import pallas as pl
from jax.experimental.pallas import tpu as pltpu
from jax.sharding import Mesh
from jax.sharding import PartitionSpec as P

ITERS = 3
STEP = 0.8
DIRS = 8
COMPS = 8
VALS = DIRS * COMPS
LANES = 128
RUN = LANES // DIRS


def cmul(left, right):
    return (left[0] * right[0] - left[1] * right[1], left[0] * right[1] + left[1] * right[0])


def cadd(left, right):
    return (left[0] + right[0], left[1] + right[1])


def adjoint(matrix):
    return [(entry[0], -entry[1]) for entry in (matrix[0], matrix[2], matrix[1], matrix[3])]


def product(left, right):
    result = []
    for row in range(2):
        for col in range(2):
            result.append(
                cadd(cmul(left[2 * row], right[col]), cmul(left[2 * row + 1], right[2 + col]))
            )
    return result


def norm_sq(matrix):
    return sum(entry[0] * entry[0] + entry[1] * entry[1] for entry in matrix)


def halves(value):
    high = value.astype(jnp.bfloat16)
    low = (value - high.astype(jnp.float32)).astype(jnp.bfloat16)
    return high, low


def select_sum(left, right, dims):
    total = None
    for part in halves(left):
        term = lax.dot_general(
            part, right, (dims, ((), ())), preferred_element_type=jnp.float32
        )
        total = term if total is None else total + term
    return total


def pick_sum(left, right, dims):
    total = None
    for part in halves(right):
        term = lax.dot_general(
            left, part, (dims, ((), ())), preferred_element_type=jnp.float32
        )
        total = term if total is None else total + term
    return total


def placed(station):
    kept = station & 0b110001111
    return kept | ((station & 0b110000) << 1) | ((station >> 2) & 0b10000)


def partials_kernel(
    gains_ref, model_ref, vis_ref, weight_ref, live_ref, first_ref, second_ref,
    out_ref, picked_ref, model_f_ref, terms_ref,
):
    base = first_ref.shape[1]
    pairs = gains_ref.shape[0]
    channels = model_ref.shape[0]
    station = placed(jnp.concatenate([first_ref[...], second_ref[...]], axis=1))
    rows = lax.broadcasted_iota(jnp.int32, (pairs, 2 * base), 0)
    hot = jnp.where(rows == station // 2, 1.0, 0.0).astype(jnp.bfloat16)
    odd = station % 2 == 1

    both = select_sum(gains_ref[...].T, hot, ((1,), (0,)))
    picked = jnp.where(odd, both[VALS:], both[:VALS])
    cuts = base // LANES
    for cut in range(2 * cuts):
        picked_ref[cut] = picked[:, cut * LANES : (cut + 1) * LANES]

    def entries(ref, at):
        comps = [ref[at, pl.ds(c, DIRS, stride=COMPS), :] for c in range(COMPS)]
        return [(comps[i], comps[i + 4]) for i in range(4)]

    live = live_ref[...].astype(jnp.float32)
    curvs = [None] * (2 * cuts)
    for cut in range(cuts):
        lanes = slice(cut * LANES, (cut + 1) * LANES)
        near = entries(picked_ref, cut)
        far = entries(picked_ref, cuts + cut)
        totals = None
        for channel in range(channels):
            model_f_ref[0] = model_ref[channel, :, lanes].astype(jnp.float32)
            model = entries(model_f_ref, 0)
            scale = weight_ref[channel : channel + 1, lanes] * live[:, lanes]
            right_a = product(model, adjoint(far))
            left_b = product(near, model)
            each = product(near, right_a)
            vis = vis_ref[channel, :, lanes]
            resid = []
            for index in range(4):
                pred_re = jnp.sum(each[index][0], axis=0, keepdims=True)
                pred_im = jnp.sum(each[index][1], axis=0, keepdims=True)
                resid.append(
                    (
                        scale * (vis[index : index + 1] - pred_re),
                        scale * (vis[index + 4 : index + 5] - pred_im),
                    )
                )
            new = (
                product(resid, adjoint(right_a)),
                product(adjoint(resid), left_b),
                scale * norm_sq(right_a),
                scale * norm_sq(left_b),
            )
            totals = new if totals is None else jax.tree.map(lambda a, b: a + b, totals, new)
        for side in range(2):
            at = side * cuts + cut
            for index, (real, imag) in enumerate(totals[side]):
                terms_ref[at, pl.ds(index, DIRS, stride=COMPS), :] = -real
                terms_ref[at, pl.ds(index + 4, DIRS, stride=COMPS), :] = -imag
            curvs[at] = totals[2 + side]

    terms = jnp.concatenate([terms_ref[at] for at in range(2 * cuts)], axis=1)
    curv = jnp.concatenate(curvs, axis=1)
    spread = jnp.concatenate([jnp.where(odd, 0.0, terms), jnp.where(odd, terms, 0.0)], axis=0)
    grads = pick_sum(hot, spread, ((1,), (1,)))
    place = station % RUN
    spread = jnp.concatenate([jnp.where(place == j, curv, 0.0) for j in range(RUN)], axis=0)
    rows = lax.broadcasted_iota(jnp.int32, (2 * pairs // RUN, 2 * base), 0)
    hot = jnp.where(rows == station // RUN, 1.0, 0.0).astype(jnp.bfloat16)
    curvs = pick_sum(hot, spread, ((1,), (1,)))
    for peer in range(pairs // RUN):
        at = peer * (RUN + 2)
        out_ref[at : at + RUN, :] = grads[peer * RUN : (peer + 1) * RUN]
        out_ref[at + RUN : at + RUN + 2, :] = curvs[2 * peer : 2 * peer + 2]


def partials(gains, model, vis, weights, live, first, second):
    pairs = gains.shape[0]
    base = first.shape[1]
    return pl.pallas_call(
        partials_kernel,
        out_shape=jax.ShapeDtypeStruct((pairs // RUN * (RUN + 2), LANES), jnp.float32),
        in_specs=[pl.BlockSpec(memory_space=pltpu.VMEM)] * 7,
        out_specs=pl.BlockSpec(memory_space=pltpu.VMEM),
        scratch_shapes=[
            pltpu.VMEM((2 * base // LANES, VALS, LANES), jnp.float32),
            pltpu.VMEM((1, VALS, LANES), jnp.float32),
            pltpu.VMEM((2 * base // LANES, VALS, LANES), jnp.float32),
        ],
        compiler_params=pltpu.CompilerParams(vmem_limit_bytes=16 * 2**20),
        name="partials",
    )(gains, model, vis, weights, live, first, second)


def peers_sum(parts_ref, rows):
    total = parts_ref[0:rows, :]
    for at in range(rows, parts_ref.shape[0], rows):
        total = total + parts_ref[at : at + rows, :]
    return total


def total_kernel(parts_ref, copies_ref):
    rows = RUN + 2
    total = peers_sum(parts_ref, rows)
    for at in range(0, copies_ref.shape[0], rows):
        copies_ref[at : at + rows, :] = total


def total(parts, peers):
    return pl.pallas_call(
        total_kernel,
        out_shape=jax.ShapeDtypeStruct((peers * (RUN + 2), LANES), jnp.float32),
        in_specs=[pl.BlockSpec(memory_space=pltpu.VMEM)],
        out_specs=pl.BlockSpec(memory_space=pltpu.VMEM),
        compiler_params=pltpu.CompilerParams(vmem_limit_bytes=16 * 2**20),
        name="total",
    )(parts)


def stepped(at_ref, parts_ref, gains_ref):
    sums = peers_sum(parts_ref, RUN + 2)
    grad = sums[:RUN]
    row = lax.broadcasted_iota(jnp.int32, (RUN, LANES), 0)
    lane = lax.broadcasted_iota(jnp.int32, (RUN, LANES), 1)
    curv = jnp.where(row < RUN // 2, sums[RUN : RUN + 1], sums[RUN + 1 : RUN + 2])
    curv = jnp.where(lane // (2 * DIRS) == row % (RUN // 2), curv, 0.0)
    source = lax.broadcasted_iota(jnp.int32, (LANES, LANES), 0)
    target = lax.broadcasted_iota(jnp.int32, (LANES, LANES), 1)
    wide = jnp.where(source % (2 * DIRS) == target // COMPS, 1.0, 0.0)
    denom = 1.0 + jnp.dot(
        curv, wide, precision=lax.Precision.HIGHEST, preferred_element_type=jnp.float32
    )
    old = gains_ref[pl.ds(pl.multiple_of(at_ref[0], RUN), RUN), :]
    return old - STEP * grad / denom, grad / jnp.sqrt(denom)


def step_kernel(at_ref, parts_ref, gains_ref, copies_ref):
    gains, _ = stepped(at_ref, parts_ref, gains_ref)
    for at in range(0, copies_ref.shape[0], RUN):
        copies_ref[at : at + RUN, :] = gains


def last_kernel(at_ref, parts_ref, gains_ref, gains_out_ref, white_ref, rows_ref):
    half = RUN // 2
    source = lax.broadcasted_iota(jnp.int32, (half, RUN), 0)
    target = lax.broadcasted_iota(jnp.int32, (half, RUN), 1)
    for value, out_ref in zip(stepped(at_ref, parts_ref, gains_ref), (gains_out_ref, white_ref)):
        rows_ref[...] = value
        turned = rows_ref[pl.ds(pl.multiple_of(at_ref[1], half), half), :].T
        out = None
        for odd in range(2):
            place = jnp.where(target == 2 * source + odd, 1.0, 0.0)
            part = jnp.dot(
                turned[odd * VALS : (odd + 1) * VALS],
                place,
                precision=lax.Precision.HIGHEST,
                preferred_element_type=jnp.float32,
            )
            out = part if out is None else out + part
        out_ref[...] = out


def step(at, parts, gains, peers):
    return pl.pallas_call(
        step_kernel,
        out_shape=jax.ShapeDtypeStruct((peers * RUN, LANES), jnp.float32),
        in_specs=[pl.BlockSpec(memory_space=pltpu.SMEM)]
        + [pl.BlockSpec(memory_space=pltpu.VMEM)] * 2,
        out_specs=pl.BlockSpec(memory_space=pltpu.VMEM),
        compiler_params=pltpu.CompilerParams(vmem_limit_bytes=16 * 2**20),
        name="step",
    )(at, parts, gains)


def last(at, parts, gains):
    return pl.pallas_call(
        last_kernel,
        out_shape=(jax.ShapeDtypeStruct((VALS, RUN), jnp.float32),) * 2,
        in_specs=[pl.BlockSpec(memory_space=pltpu.SMEM)]
        + [pl.BlockSpec(memory_space=pltpu.VMEM)] * 2,
        out_specs=(pl.BlockSpec(memory_space=pltpu.VMEM),) * 2,
        scratch_shapes=[pltpu.VMEM((RUN, LANES), jnp.float32)],
        compiler_params=pltpu.CompilerParams(vmem_limit_bytes=16 * 2**20),
        name="last",
    )(at, parts, gains)


def exchange(rows, axes, peers):
    count = rows.shape[0]
    sent = rows.reshape(peers, 1, count // peers * LANES)
    return lax.all_to_all(sent, axes, 0, 0).reshape(count, LANES)


def per_device(model, vis, weights, antenna1, antenna2, live, gains):
    base = antenna1.shape[0]
    channels = model.shape[1]
    owned = gains.shape[3]
    near, far = ("x", "z0", "core"), ("y", "z1")
    model = model.reshape(channels, VALS, base)
    vis, weights = vis[0], weights[0]
    first, second, live = (a.reshape(1, base) for a in (antenna1, antenna2, live))
    mine = gains.reshape(VALS, owned).T.reshape(1, owned * VALS // LANES, LANES)
    mine = jnp.broadcast_to(mine, (32,) + mine.shape[1:]).reshape(-1, LANES)
    full = exchange(mine, near + ("z1",), 32)
    place = lax.axis_index(near)
    at = jnp.stack([place * RUN, lax.axis_index("z1") * (RUN // 2)]).astype(jnp.int32)
    for turn in range(ITERS):
        sent = partials(full, model, vis, weights, live, first, second)
        sent = total(exchange(sent, near, 16), 16)
        sums = exchange(sent, far, 16)
        if turn < ITERS - 1:
            full = exchange(step(at, sums, full, 16), near, 16)
    return tuple(out.reshape(gains.shape) for out in last(at, sums, full))


def solution(mesh):
    fine = Mesh(mesh.devices.reshape(8, 4, 2, 2, 2, 2), ("y", "x", "z1", "z0", "core", "chan"))
    bl = ("x", "z1", "z0", "core")
    return jax.shard_map(
        per_device,
        mesh=fine,
        in_specs=(
            P("y", "chan", None, None, bl),
            P("y", "chan", None, bl),
            P("y", "chan", bl),
            P(bl),
            P(bl),
            P(bl),
            P("chan", None, None, bl),
        ),
        out_specs=(P("chan", None, None, bl), P("chan", None, None, bl)),
        check_vma=False,
    )
```

```python
import functools

import jax
import jax.numpy as jnp
from jax import lax
from jax.experimental import pallas as pl
from jax.experimental.pallas import tpu as pltpu
from jax.sharding import Mesh
from jax.sharding import PartitionSpec as P

ITERS = 3
STEP = 0.8
DIRS = 8
COMPS = 8
VALS = DIRS * COMPS
LANES = 128
RUN = LANES // DIRS


def cmul(left, right):
    return (left[0] * right[0] - left[1] * right[1], left[0] * right[1] + left[1] * right[0])


def cadd(left, right):
    return (left[0] + right[0], left[1] + right[1])


def adjoint(matrix):
    return [(entry[0], -entry[1]) for entry in (matrix[0], matrix[2], matrix[1], matrix[3])]


def product(left, right):
    result = []
    for row in range(2):
        for col in range(2):
            result.append(
                cadd(cmul(left[2 * row], right[col]), cmul(left[2 * row + 1], right[2 + col]))
            )
    return result


def norm_sq(matrix):
    return sum(entry[0] * entry[0] + entry[1] * entry[1] for entry in matrix)


def halves(value):
    high = value.astype(jnp.bfloat16)
    low = (value - high.astype(jnp.float32)).astype(jnp.bfloat16)
    return high, low


def select_sum(left, right, dims):
    total = None
    for part in halves(left):
        term = lax.dot_general(
            part, right, (dims, ((), ())), preferred_element_type=jnp.float32
        )
        total = term if total is None else total + term
    return total


def pick_sum(left, right, dims):
    total = None
    for part in halves(right):
        term = lax.dot_general(
            left, part, (dims, ((), ())), preferred_element_type=jnp.float32
        )
        total = term if total is None else total + term
    return total


def placed(station):
    kept = station & 0b110001111
    return kept | ((station & 0b110000) << 1) | ((station >> 2) & 0b10000)


def in_vmem(count):
    return [pl.BlockSpec(memory_space=pltpu.VMEM)] * count


PARAMS = pltpu.CompilerParams(vmem_limit_bytes=16 * 2**20)


def pack_kernel(model_ref, vis_ref, weight_ref, live_ref, gains_ref, data_ref, copies_ref):
    channels, base = weight_ref.shape
    cuts = base // LANES
    live = live_ref[...].astype(jnp.float32)
    scales = []
    for part in range(channels * cuts):
        channel, cut = divmod(part, cuts)
        lanes = slice(cut * LANES, (cut + 1) * LANES)
        at = part * (VALS + COMPS)
        data_ref[at : at + VALS, :] = model_ref[channel, :, lanes].astype(jnp.float32)
        data_ref[at + VALS : at + VALS + COMPS, :] = vis_ref[channel, :, lanes]
        scales.append(weight_ref[channel : channel + 1, lanes] * live[:, lanes])
    at = len(scales) * (VALS + COMPS)
    spare = data_ref.shape[0] - at - len(scales)
    scales.append(jnp.zeros((spare, LANES), jnp.float32))
    data_ref[at:, :] = jnp.concatenate(scales, axis=0)

    owned = gains_ref.shape[1]
    target = lax.broadcasted_iota(jnp.int32, (owned // 2, owned), 0)
    source = lax.broadcasted_iota(jnp.int32, (owned // 2, owned), 1)
    mine = jnp.concatenate(
        [
            lax.dot_general(
                jnp.where(source == 2 * target + odd, 1.0, 0.0),
                gains_ref[...],
                (((1,), (1,)), ((), ())),
                precision=lax.Precision.HIGHEST,
                preferred_element_type=jnp.float32,
            )
            for odd in range(2)
        ],
        axis=1,
    )
    for at in range(0, copies_ref.shape[0], owned // 2):
        copies_ref[at : at + owned // 2, :] = mine


def pack(model, vis, weights, live, gains, peers):
    channels, base = weights.shape
    parts = channels * base // LANES
    rows = parts * (VALS + COMPS) + -(-parts // 8) * 8
    owned = gains.shape[1]
    return pl.pallas_call(
        pack_kernel,
        out_shape=(
            jax.ShapeDtypeStruct((rows, LANES), jnp.float32),
            jax.ShapeDtypeStruct((peers * owned // 2, LANES), jnp.float32),
        ),
        in_specs=in_vmem(5),
        out_specs=tuple(in_vmem(2)),
        compiler_params=PARAMS,
        name="pack",
    )(model, vis, weights, live, gains)


def partials_kernel(
    run, channels, gains_ref, data_ref, first_ref, second_ref, out_ref, picked_ref, terms_ref
):
    base = first_ref.shape[1]
    pairs = gains_ref.shape[0]
    times = data_ref.shape[0]
    cuts = base // LANES
    station = placed(jnp.concatenate([first_ref[...], second_ref[...]], axis=1))
    rows = lax.broadcasted_iota(jnp.int32, (pairs, 2 * base), 0)
    hot = jnp.where(rows == station // 2, 1.0, 0.0).astype(jnp.bfloat16)
    odd = station % 2 == 1

    both = select_sum(gains_ref[...].T, hot, ((1,), (0,)))
    picked = jnp.where(odd, both[VALS:], both[:VALS])
    for cut in range(2 * cuts):
        picked_ref[cut] = picked[:, cut * LANES : (cut + 1) * LANES]

    def entries(ref, outer, at):
        comps = [ref[outer, pl.ds(at + c, DIRS, stride=COMPS), :] for c in range(COMPS)]
        return [(comps[i], comps[i + 4]) for i in range(4)]

    curvs = [None] * (2 * cuts)
    for cut in range(cuts):
        near = entries(picked_ref, cut, 0)
        far = entries(picked_ref, cuts + cut, 0)

        def at_time(time, totals, cut=cut, near=near, far=far):
            for channel in range(channels):
                part = channel * cuts + cut
                at = part * (VALS + COMPS)
                model = entries(data_ref, time, at)
                vis = data_ref[time, at + VALS : at + VALS + COMPS, :]
                row = channels * cuts * (VALS + COMPS) + part
                scale = data_ref[time, row : row + 1, :]
                right_a = product(model, adjoint(far))
                left_b = product(near, model)
                each = product(near, right_a)
                resid = []
                for index in range(4):
                    pred_re = jnp.sum(each[index][0], axis=0, keepdims=True)
                    pred_im = jnp.sum(each[index][1], axis=0, keepdims=True)
                    resid.append(
                        (
                            scale * (vis[index : index + 1] - pred_re),
                            scale * (vis[index + 4 : index + 5] - pred_im),
                        )
                    )
                new = (
                    product(resid, adjoint(right_a)),
                    product(adjoint(resid), left_b),
                    scale * norm_sq(right_a),
                    scale * norm_sq(left_b),
                )
                totals = new if totals is None else jax.tree.map(jnp.add, totals, new)
            return totals

        totals = at_time(0, None)
        if times > 1:
            totals = lax.fori_loop(1, times, at_time, totals)
        for side in range(2):
            at = side * cuts + cut
            for index, (real, imag) in enumerate(totals[side]):
                terms_ref[at, pl.ds(index, DIRS, stride=COMPS), :] = -real
                terms_ref[at, pl.ds(index + 4, DIRS, stride=COMPS), :] = -imag
            curvs[at] = totals[2 + side]

    terms = jnp.concatenate([terms_ref[at] for at in range(2 * cuts)], axis=1)
    curv = jnp.concatenate(curvs, axis=1)
    spread = jnp.concatenate([jnp.where(odd, 0.0, terms), jnp.where(odd, terms, 0.0)], axis=0)
    grads = pick_sum(hot, spread, ((1,), (1,)))
    place = station % RUN
    spread = jnp.concatenate([jnp.where(place == j, curv, 0.0) for j in range(RUN)], axis=0)
    rows = lax.broadcasted_iota(jnp.int32, (2 * pairs // RUN, 2 * base), 0)
    hot = jnp.where(rows == station // RUN, 1.0, 0.0).astype(jnp.bfloat16)
    curvs = pick_sum(hot, spread, ((1,), (1,)))
    extra = run // 8
    for peer in range(pairs // run):
        at = peer * (run + extra)
        out_ref[at : at + run, :] = grads[peer * run : (peer + 1) * run]
        out_ref[at + run : at + run + extra, :] = curvs[peer * extra : (peer + 1) * extra]


def partials(run, channels, gains, data, first, second):
    pairs = gains.shape[0]
    base = first.shape[1]
    return pl.pallas_call(
        functools.partial(partials_kernel, run, channels),
        out_shape=jax.ShapeDtypeStruct((pairs // 8 * 9, LANES), jnp.float32),
        in_specs=in_vmem(4),
        out_specs=in_vmem(1)[0],
        scratch_shapes=[pltpu.VMEM((2 * base // LANES, VALS, LANES), jnp.float32)] * 2,
        compiler_params=PARAMS,
        name="partials",
    )(gains, data, first, second)


def peers_sum(parts_ref, rows):
    total = parts_ref[0:rows, :]
    for at in range(rows, parts_ref.shape[0], rows):
        total = total + parts_ref[at : at + rows, :]
    return total


def total_kernel(rows, parts_ref, copies_ref):
    total = peers_sum(parts_ref, rows)
    for at in range(0, copies_ref.shape[0], rows):
        copies_ref[at : at + rows, :] = total


def total(run, parts, peers):
    rows = run // 8 * 9
    return pl.pallas_call(
        functools.partial(total_kernel, rows),
        out_shape=jax.ShapeDtypeStruct((peers * rows, LANES), jnp.float32),
        in_specs=in_vmem(1),
        out_specs=in_vmem(1)[0],
        compiler_params=PARAMS,
        name="total",
    )(parts)


def stepped(run, at_ref, parts_ref, gains_ref):
    sums = peers_sum(parts_ref, run // 8 * 9)
    grad = sums[:run]
    row = lax.broadcasted_iota(jnp.int32, (run, LANES), 0)
    lane = lax.broadcasted_iota(jnp.int32, (run, LANES), 1)
    curv = sums[run : run + 1]
    for extra in range(1, run // 8):
        curv = jnp.where(row < 8 * extra, curv, sums[run + extra : run + extra + 1])
    curv = jnp.where(lane // (2 * DIRS) == row % 8, curv, 0.0)
    source = lax.broadcasted_iota(jnp.int32, (LANES, LANES), 0)
    target = lax.broadcasted_iota(jnp.int32, (LANES, LANES), 1)
    wide = jnp.where(source % (2 * DIRS) == target // COMPS, 1.0, 0.0)
    denom = 1.0 + jnp.dot(
        curv, wide, precision=lax.Precision.HIGHEST, preferred_element_type=jnp.float32
    )
    old = gains_ref[pl.ds(pl.multiple_of(at_ref[0], run), run), :]
    return old - STEP * grad / denom, grad / jnp.sqrt(denom)


def step_kernel(run, at_ref, parts_ref, gains_ref, copies_ref):
    gains, _ = stepped(run, at_ref, parts_ref, gains_ref)
    for at in range(0, copies_ref.shape[0], run):
        copies_ref[at : at + run, :] = gains


def last_kernel(run, at_ref, parts_ref, gains_ref, gains_out_ref, white_ref):
    owned = 2 * run
    source = lax.broadcasted_iota(jnp.int32, (run, owned), 0)
    target = lax.broadcasted_iota(jnp.int32, (run, owned), 1)
    results = stepped(run, at_ref, parts_ref, gains_ref)
    for value, out_ref in zip(results, (gains_out_ref, white_ref)):
        turned = value.T
        out = None
        for odd in range(2):
            place = jnp.where(target == 2 * source + odd, 1.0, 0.0)
            part = jnp.dot(
                turned[odd * VALS : (odd + 1) * VALS],
                place,
                precision=lax.Precision.HIGHEST,
                preferred_element_type=jnp.float32,
            )
            out = part if out is None else out + part
        out_ref[...] = out


def step(run, at, parts, gains):
    return pl.pallas_call(
        functools.partial(step_kernel, run),
        out_shape=jax.ShapeDtypeStruct(gains.shape, jnp.float32),
        in_specs=[pl.BlockSpec(memory_space=pltpu.SMEM)] + in_vmem(2),
        out_specs=in_vmem(1)[0],
        compiler_params=PARAMS,
        name="step",
    )(at, parts, gains)


def last(run, at, parts, gains):
    return pl.pallas_call(
        functools.partial(last_kernel, run),
        out_shape=(jax.ShapeDtypeStruct((VALS, 2 * run), jnp.float32),) * 2,
        in_specs=[pl.BlockSpec(memory_space=pltpu.SMEM)] + in_vmem(2),
        out_specs=tuple(in_vmem(2)),
        compiler_params=PARAMS,
        name="last",
    )(at, parts, gains)


def exchange(rows, axes, peers):
    count = rows.shape[0]
    sent = rows.reshape(peers, 1, count // peers * LANES)
    return lax.all_to_all(sent, axes, 0, 0).reshape(count, LANES)


def per_device(model, vis, weights, antenna1, antenna2, live, gains):
    base = antenna1.shape[0]
    channels = model.shape[1]
    near, far = ("x", "z0", "core"), ("y", "z1")
    wide = near + ("z1",)
    first, second, live = (a.reshape(1, base) for a in (antenna1, antenna2, live))
    data, copies = pack(
        model.reshape(channels, VALS, base), vis[0], weights[0], live,
        gains.reshape(VALS, gains.shape[3]), 32,
    )
    every = lax.all_gather(data, "y")
    full = exchange(copies, wide, 32)

    at = (lax.axis_index(near) * 16).reshape(1).astype(jnp.int32)
    sent = partials(16, channels, full, data[None], first, second)
    sent = total(16, exchange(sent, near, 16), 16)
    full = exchange(step(16, at, exchange(sent, far, 16), full), near, 16)

    at = (lax.axis_index(wide) * 8).reshape(1).astype(jnp.int32)
    for turn in range(1, ITERS):
        sums = exchange(partials(8, channels, full, every, first, second), wide, 32)
        if turn < ITERS - 1:
            full = exchange(step(8, at, sums, full), wide, 32)
    return tuple(out.reshape(gains.shape) for out in last(8, at, sums, full))


def solution(mesh):
    fine = Mesh(mesh.devices.reshape(8, 4, 2, 2, 2, 2), ("y", "x", "z1", "z0", "core", "chan"))
    bl = ("x", "z1", "z0", "core")
    return jax.shard_map(
        per_device,
        mesh=fine,
        in_specs=(
            P("y", "chan", None, None, bl),
            P("y", "chan", None, bl),
            P("y", "chan", bl),
            P(bl),
            P(bl),
            P(bl),
            P("chan", None, None, bl),
        ),
        out_specs=(P("chan", None, None, bl), P("chan", None, None, bl)),
        check_vma=False,
    )
```

```python
import functools

import jax
import jax.numpy as jnp
from jax import lax
from jax.experimental import pallas as pl
from jax.experimental.pallas import tpu as pltpu
from jax.sharding import Mesh
from jax.sharding import PartitionSpec as P

ITERS = 3
STEP = 0.8
DIRS = 8
COMPS = 8
VALS = DIRS * COMPS
LANES = 128
RUN = LANES // DIRS


def cmul(left, right):
    return (left[0] * right[0] - left[1] * right[1], left[0] * right[1] + left[1] * right[0])


def cadd(left, right):
    return (left[0] + right[0], left[1] + right[1])


def adjoint(matrix):
    return [(entry[0], -entry[1]) for entry in (matrix[0], matrix[2], matrix[1], matrix[3])]


def product(left, right):
    result = []
    for row in range(2):
        for col in range(2):
            result.append(
                cadd(cmul(left[2 * row], right[col]), cmul(left[2 * row + 1], right[2 + col]))
            )
    return result


def norm_sq(matrix):
    return sum(entry[0] * entry[0] + entry[1] * entry[1] for entry in matrix)


def halves(value):
    high = value.astype(jnp.bfloat16)
    low = (value - high.astype(jnp.float32)).astype(jnp.bfloat16)
    return high, low


def select_sum(left, right, dims):
    rows = left.shape[0]
    both = lax.dot_general(
        jnp.concatenate(halves(left), axis=0), right, (dims, ((), ())),
        preferred_element_type=jnp.float32,
    )
    return both[:rows] + both[rows:]


def pick_sum(left, right, dims):
    rows = right.shape[0]
    both = lax.dot_general(
        left, jnp.concatenate(halves(right), axis=0), (dims, ((), ())),
        preferred_element_type=jnp.float32,
    )
    return both[:, :rows] + both[:, rows:]


def placed(station):
    kept = station & 0b110001111
    return kept | ((station & 0b110000) << 1) | ((station >> 2) & 0b10000)


def partials_kernel(
    gains_ref, model_ref, vis_ref, weight_ref, live_ref, first_ref, second_ref,
    out_ref, picked_ref, model_f_ref, terms_ref,
):
    base = first_ref.shape[1]
    pairs = gains_ref.shape[0]
    channels = model_ref.shape[0]
    station = placed(jnp.concatenate([first_ref[...], second_ref[...]], axis=1))
    rows = lax.broadcasted_iota(jnp.int32, (pairs, 2 * base), 0)
    hot = jnp.where(rows == station // 2, 1.0, 0.0).astype(jnp.bfloat16)
    odd = station % 2 == 1

    both = select_sum(gains_ref[...].T, hot, ((1,), (0,)))
    picked = jnp.where(odd, both[VALS:], both[:VALS])
    cuts = base // LANES
    for cut in range(2 * cuts):
        picked_ref[cut] = picked[:, cut * LANES : (cut + 1) * LANES]

    def entries(ref, at):
        comps = [ref[at, pl.ds(c, DIRS, stride=COMPS), :] for c in range(COMPS)]
        return [(comps[i], comps[i + 4]) for i in range(4)]

    live = live_ref[...].astype(jnp.float32)
    curvs = [None] * (2 * cuts)
    for cut in range(cuts):
        lanes = slice(cut * LANES, (cut + 1) * LANES)
        near = entries(picked_ref, cut)
        far = entries(picked_ref, cuts + cut)
        totals = None
        for channel in range(channels):
            model_f_ref[0] = model_ref[channel, :, lanes].astype(jnp.float32)
            model = entries(model_f_ref, 0)
            scale = weight_ref[channel : channel + 1, lanes] * live[:, lanes]
            right_a = product(model, adjoint(far))
            left_b = product(near, model)
            each = product(near, right_a)
            vis = vis_ref[channel, :, lanes]
            resid = []
            for index in range(4):
                pred_re = jnp.sum(each[index][0], axis=0, keepdims=True)
                pred_im = jnp.sum(each[index][1], axis=0, keepdims=True)
                resid.append(
                    (
                        scale * (vis[index : index + 1] - pred_re),
                        scale * (vis[index + 4 : index + 5] - pred_im),
                    )
                )
            new = (
                product(resid, adjoint(right_a)),
                product(adjoint(resid), left_b),
                scale * norm_sq(right_a),
                scale * norm_sq(left_b),
            )
            totals = new if totals is None else jax.tree.map(lambda a, b: a + b, totals, new)
        for side in range(2):
            at = side * cuts + cut
            for index, (real, imag) in enumerate(totals[side]):
                terms_ref[at, pl.ds(index, DIRS, stride=COMPS), :] = -real
                terms_ref[at, pl.ds(index + 4, DIRS, stride=COMPS), :] = -imag
            curvs[at] = totals[2 + side]

    terms = jnp.concatenate([terms_ref[at] for at in range(2 * cuts)], axis=1)
    curv = jnp.concatenate(curvs, axis=1)
    spread = jnp.concatenate([jnp.where(odd, 0.0, terms), jnp.where(odd, terms, 0.0)], axis=0)
    grads = pick_sum(hot, spread, ((1,), (1,)))
    wide = jnp.concatenate([curv] * RUN, axis=0)
    seat = lax.broadcasted_iota(jnp.int32, wide.shape, 0) // DIRS
    spread = jnp.where(seat == station % RUN, wide, 0.0)
    rows = lax.broadcasted_iota(jnp.int32, (2 * pairs // RUN, 2 * base), 0)
    hot = jnp.where(rows == station // RUN, 1.0, 0.0).astype(jnp.bfloat16)
    curvs = pick_sum(hot, spread, ((1,), (1,)))
    for peer in range(pairs // RUN):
        at = peer * (RUN + 2)
        out_ref[at : at + RUN, :] = grads[peer * RUN : (peer + 1) * RUN]
        out_ref[at + RUN : at + RUN + 2, :] = curvs[2 * peer : 2 * peer + 2]


def partials(gains, model, vis, weights, live, first, second):
    pairs = gains.shape[0]
    base = first.shape[1]
    return pl.pallas_call(
        partials_kernel,
        out_shape=jax.ShapeDtypeStruct((pairs // RUN * (RUN + 2), LANES), jnp.float32),
        in_specs=[pl.BlockSpec(memory_space=pltpu.VMEM)] * 7,
        out_specs=pl.BlockSpec(memory_space=pltpu.VMEM),
        scratch_shapes=[
            pltpu.VMEM((2 * base // LANES, VALS, LANES), jnp.float32),
            pltpu.VMEM((1, VALS, LANES), jnp.float32),
            pltpu.VMEM((2 * base // LANES, VALS, LANES), jnp.float32),
        ],
        compiler_params=pltpu.CompilerParams(vmem_limit_bytes=16 * 2**20),
        name="partials",
    )(gains, model, vis, weights, live, first, second)


def peers_sum(parts_ref, rows):
    total = parts_ref[0:rows, :]
    for at in range(rows, parts_ref.shape[0], rows):
        total = total + parts_ref[at : at + rows, :]
    return total


def total_kernel(parts_ref, copies_ref):
    rows = RUN + 2
    total = peers_sum(parts_ref, rows)
    for at in range(0, copies_ref.shape[0], rows):
        copies_ref[at : at + rows, :] = total


def total(parts, peers):
    return pl.pallas_call(
        total_kernel,
        out_shape=jax.ShapeDtypeStruct((peers * (RUN + 2), LANES), jnp.float32),
        in_specs=[pl.BlockSpec(memory_space=pltpu.VMEM)],
        out_specs=pl.BlockSpec(memory_space=pltpu.VMEM),
        compiler_params=pltpu.CompilerParams(vmem_limit_bytes=16 * 2**20),
        name="total",
    )(parts)


def stepped(at_ref, parts_ref, gains_ref):
    sums = peers_sum(parts_ref, RUN + 2)
    grad = sums[:RUN]
    row = lax.broadcasted_iota(jnp.int32, (RUN, LANES), 0)
    lane = lax.broadcasted_iota(jnp.int32, (RUN, LANES), 1)
    curv = jnp.where(row < RUN // 2, sums[RUN : RUN + 1], sums[RUN + 1 : RUN + 2])
    curv = jnp.where(lane // (2 * DIRS) == row % (RUN // 2), curv, 0.0)
    source = lax.broadcasted_iota(jnp.int32, (LANES, LANES), 0)
    target = lax.broadcasted_iota(jnp.int32, (LANES, LANES), 1)
    wide = jnp.where(source % (2 * DIRS) == target // COMPS, 1.0, 0.0)
    denom = 1.0 + jnp.dot(
        curv, wide, precision=lax.Precision.HIGHEST, preferred_element_type=jnp.float32
    )
    old = gains_ref[pl.ds(pl.multiple_of(at_ref[0], RUN), RUN), :]
    return old - STEP * grad / denom, grad / jnp.sqrt(denom)


def step_kernel(at_ref, parts_ref, gains_ref, copies_ref):
    gains, _ = stepped(at_ref, parts_ref, gains_ref)
    for at in range(0, copies_ref.shape[0], RUN):
        copies_ref[at : at + RUN, :] = gains


def last_kernel(at_ref, half_ref, parts_ref, gains_ref, gains_out_ref, white_ref):
    owned = gains_out_ref.shape[1]
    source = lax.broadcasted_iota(jnp.int32, (RUN, owned), 0) - half_ref[0]
    target = lax.broadcasted_iota(jnp.int32, (RUN, owned), 1)
    results = stepped(at_ref, parts_ref, gains_ref)
    for value, out_ref in zip(results, (gains_out_ref, white_ref)):
        out = None
        for odd in range(2):
            part = lax.dot_general(
                value[:, odd * VALS : (odd + 1) * VALS],
                jnp.where(target == 2 * source + odd, 1.0, 0.0),
                (((0,), (0,)), ((), ())),
                precision=lax.Precision.HIGHEST,
                preferred_element_type=jnp.float32,
            )
            out = part if out is None else out + part
        out_ref[...] = out


def step(at, parts, gains, peers):
    return pl.pallas_call(
        step_kernel,
        out_shape=jax.ShapeDtypeStruct((peers * RUN, LANES), jnp.float32),
        in_specs=[pl.BlockSpec(memory_space=pltpu.SMEM)]
        + [pl.BlockSpec(memory_space=pltpu.VMEM)] * 2,
        out_specs=pl.BlockSpec(memory_space=pltpu.VMEM),
        compiler_params=pltpu.CompilerParams(vmem_limit_bytes=16 * 2**20),
        name="step",
    )(at, parts, gains)


def last(at, half, parts, gains, owned):
    return pl.pallas_call(
        last_kernel,
        out_shape=(jax.ShapeDtypeStruct((VALS, owned), jnp.float32),) * 2,
        in_specs=[pl.BlockSpec(memory_space=pltpu.SMEM)] * 2 + [pl.BlockSpec(memory_space=pltpu.VMEM)] * 2,
        out_specs=tuple([pl.BlockSpec(memory_space=pltpu.VMEM)] * 2),
        compiler_params=pltpu.CompilerParams(vmem_limit_bytes=16 * 2**20),
        name="last",
    )(at, half, parts, gains)


def exchange(rows, axes, peers):
    count = rows.shape[0]
    sent = rows.reshape(peers, 1, count // peers * LANES)
    return lax.all_to_all(sent, axes, 0, 0).reshape(count, LANES)


def per_device(model, vis, weights, antenna1, antenna2, live, gains):
    base = antenna1.shape[0]
    channels = model.shape[1]
    owned = gains.shape[3]
    near, far = ("x", "z0", "core"), ("z1", "y")
    model = model.reshape(channels, VALS, base)
    vis, weights = vis[0], weights[0]
    first, second, live = (a.reshape(1, base) for a in (antenna1, antenna2, live))
    mine = gains.reshape(VALS, owned).T.reshape(1, owned * VALS // LANES, LANES)
    mine = jnp.broadcast_to(mine, (32,) + mine.shape[1:]).reshape(-1, LANES)
    full = exchange(mine, near + ("z1",), 32)
    at = (lax.axis_index(near) * RUN).reshape(1).astype(jnp.int32)
    half = (lax.axis_index("z1") * (RUN // 2)).reshape(1).astype(jnp.int32)
    for turn in range(ITERS):
        sent = partials(full, model, vis, weights, live, first, second)
        sent = total(exchange(sent, near, 16), 16)
        sums = exchange(sent, far, 16)
        if turn < ITERS - 1:
            full = exchange(step(at, sums, full, 16), near, 16)
    return tuple(out.reshape(gains.shape) for out in last(at, half, sums, full, owned))


def solution(mesh):
    fine = Mesh(mesh.devices.reshape(8, 4, 2, 2, 2, 2), ("y", "x", "z1", "z0", "core", "chan"))
    bl = ("x", "z1", "z0", "core")
    return jax.shard_map(
        per_device,
        mesh=fine,
        in_specs=(
            P("y", "chan", None, None, bl),
            P("y", "chan", None, bl),
            P("y", "chan", bl),
            P(bl),
            P(bl),
            P(bl),
            P("chan", None, None, bl),
        ),
        out_specs=(P("chan", None, None, bl), P("chan", None, None, bl)),
        check_vma=False,
    )
```

```python
import functools

import jax
import jax.numpy as jnp
from jax import lax
from jax.experimental import pallas as pl
from jax.experimental.pallas import tpu as pltpu
from jax.sharding import Mesh
from jax.sharding import PartitionSpec as P

ITERS = 3
STEP = 0.8
DIRS = 8
COMPS = 8
VALS = DIRS * COMPS
LANES = 128
RUN = LANES // DIRS
NEAR = ("x", "z0", "core")
FAR = ("z1", "y")


def cmul(left, right):
    return (left[0] * right[0] - left[1] * right[1], left[0] * right[1] + left[1] * right[0])


def cadd(left, right):
    return (left[0] + right[0], left[1] + right[1])


def adjoint(matrix):
    return [(entry[0], -entry[1]) for entry in (matrix[0], matrix[2], matrix[1], matrix[3])]


def product(left, right):
    result = []
    for row in range(2):
        for col in range(2):
            result.append(
                cadd(cmul(left[2 * row], right[col]), cmul(left[2 * row + 1], right[2 + col]))
            )
    return result


def norm_sq(matrix):
    return sum(entry[0] * entry[0] + entry[1] * entry[1] for entry in matrix)


def halves(value):
    high = value.astype(jnp.bfloat16)
    low = (value - high.astype(jnp.float32)).astype(jnp.bfloat16)
    return high, low


def select_sum(left, right, dims):
    rows = left.shape[0]
    both = lax.dot_general(
        jnp.concatenate(halves(left), axis=0), right, (dims, ((), ())),
        preferred_element_type=jnp.float32,
    )
    return both[:rows] + both[rows:]


def pick_sum(left, right, dims):
    rows = right.shape[0]
    both = lax.dot_general(
        left, jnp.concatenate(halves(right), axis=0), (dims, ((), ())),
        preferred_element_type=jnp.float32,
    )
    return both[:, :rows] + both[:, rows:]


def placed(station):
    kept = station & 0b110001111
    return kept | ((station & 0b110000) << 1) | ((station >> 2) & 0b10000)


def partials_kernel(
    gains_ref, model_ref, vis_ref, weight_ref, live_ref, first_ref, second_ref,
    out_ref, picked_ref, model_f_ref, terms_ref,
):
    base = first_ref.shape[1]
    pairs = gains_ref.shape[0]
    channels = model_ref.shape[0]
    station = placed(jnp.concatenate([first_ref[...], second_ref[...]], axis=1))
    rows = lax.broadcasted_iota(jnp.int32, (pairs, 2 * base), 0)
    hot = jnp.where(rows == station // 2, 1.0, 0.0).astype(jnp.bfloat16)
    odd = station % 2 == 1

    both = select_sum(gains_ref[...].T, hot, ((1,), (0,)))
    picked = jnp.where(odd, both[VALS:], both[:VALS])
    cuts = base // LANES
    for cut in range(2 * cuts):
        picked_ref[cut] = picked[:, cut * LANES : (cut + 1) * LANES]

    def entries(ref, at):
        comps = [ref[at, pl.ds(c, DIRS, stride=COMPS), :] for c in range(COMPS)]
        return [(comps[i], comps[i + 4]) for i in range(4)]

    live = live_ref[...].astype(jnp.float32)
    curvs = [None] * (2 * cuts)
    for cut in range(cuts):
        lanes = slice(cut * LANES, (cut + 1) * LANES)
        near = entries(picked_ref, cut)
        far = entries(picked_ref, cuts + cut)
        totals = None
        for channel in range(channels):
            model_f_ref[0] = model_ref[channel, :, lanes].astype(jnp.float32)
            model = entries(model_f_ref, 0)
            scale = weight_ref[channel : channel + 1, lanes] * live[:, lanes]
            right_a = product(model, adjoint(far))
            left_b = product(near, model)
            each = product(near, right_a)
            vis = vis_ref[channel, :, lanes]
            resid = []
            for index in range(4):
                pred_re = jnp.sum(each[index][0], axis=0, keepdims=True)
                pred_im = jnp.sum(each[index][1], axis=0, keepdims=True)
                resid.append(
                    (
                        scale * (vis[index : index + 1] - pred_re),
                        scale * (vis[index + 4 : index + 5] - pred_im),
                    )
                )
            new = (
                product(resid, adjoint(right_a)),
                product(adjoint(resid), left_b),
                scale * norm_sq(right_a),
                scale * norm_sq(left_b),
            )
            totals = new if totals is None else jax.tree.map(lambda a, b: a + b, totals, new)
        for side in range(2):
            at = side * cuts + cut
            for index, (real, imag) in enumerate(totals[side]):
                terms_ref[at, pl.ds(index, DIRS, stride=COMPS), :] = -real
                terms_ref[at, pl.ds(index + 4, DIRS, stride=COMPS), :] = -imag
            curvs[at] = totals[2 + side]

    terms = jnp.concatenate([terms_ref[at] for at in range(2 * cuts)], axis=1)
    curv = jnp.concatenate(curvs, axis=1)
    spread = jnp.concatenate([jnp.where(odd, 0.0, terms), jnp.where(odd, terms, 0.0)], axis=0)
    grads = pick_sum(hot, spread, ((1,), (1,)))
    wide = jnp.concatenate([curv] * RUN, axis=0)
    seat = lax.broadcasted_iota(jnp.int32, wide.shape, 0) // DIRS
    spread = jnp.where(seat == station % RUN, wide, 0.0)
    rows = lax.broadcasted_iota(jnp.int32, (2 * pairs // RUN, 2 * base), 0)
    hot = jnp.where(rows == station // RUN, 1.0, 0.0).astype(jnp.bfloat16)
    curvs = pick_sum(hot, spread, ((1,), (1,)))
    for peer in range(pairs // RUN):
        at = peer * (RUN + 2)
        out_ref[at : at + RUN, :] = grads[peer * RUN : (peer + 1) * RUN]
        out_ref[at + RUN : at + RUN + 2, :] = curvs[2 * peer : 2 * peer + 2]


def partials(gains, model, vis, weights, live, first, second):
    pairs = gains.shape[0]
    base = first.shape[1]
    return pl.pallas_call(
        partials_kernel,
        out_shape=jax.ShapeDtypeStruct((pairs // RUN * (RUN + 2), LANES), jnp.float32),
        in_specs=[pl.BlockSpec(memory_space=pltpu.VMEM)] * 7,
        out_specs=pl.BlockSpec(memory_space=pltpu.VMEM),
        scratch_shapes=[
            pltpu.VMEM((2 * base // LANES, VALS, LANES), jnp.float32),
            pltpu.VMEM((1, VALS, LANES), jnp.float32),
            pltpu.VMEM((2 * base // LANES, VALS, LANES), jnp.float32),
        ],
        compiler_params=pltpu.CompilerParams(vmem_limit_bytes=16 * 2**20),
        name="partials",
    )(gains, model, vis, weights, live, first, second)


def peers_sum(parts_ref, rows):
    total = parts_ref[0:rows, :]
    for at in range(rows, parts_ref.shape[0], rows):
        total = total + parts_ref[at : at + rows, :]
    return total


def total_kernel(parts_ref, copies_ref):
    rows = RUN + 2
    total = peers_sum(parts_ref, rows)
    for at in range(0, copies_ref.shape[0], rows):
        copies_ref[at : at + rows, :] = total


def total(parts, peers):
    return pl.pallas_call(
        total_kernel,
        out_shape=jax.ShapeDtypeStruct((peers * (RUN + 2), LANES), jnp.float32),
        in_specs=[pl.BlockSpec(memory_space=pltpu.VMEM)],
        out_specs=pl.BlockSpec(memory_space=pltpu.VMEM),
        compiler_params=pltpu.CompilerParams(vmem_limit_bytes=16 * 2**20),
        name="total",
    )(parts)


def stepped(parts_ref, gains_ref):
    sums = peers_sum(parts_ref, RUN + 2)
    grad = sums[:RUN]
    row = lax.broadcasted_iota(jnp.int32, (RUN, LANES), 0)
    lane = lax.broadcasted_iota(jnp.int32, (RUN, LANES), 1)
    curv = jnp.where(row < RUN // 2, sums[RUN : RUN + 1], sums[RUN + 1 : RUN + 2])
    curv = jnp.where(lane // (2 * DIRS) == row % (RUN // 2), curv, 0.0)
    source = lax.broadcasted_iota(jnp.int32, (LANES, LANES), 0)
    target = lax.broadcasted_iota(jnp.int32, (LANES, LANES), 1)
    wide = jnp.where(source % (2 * DIRS) == target // COMPS, 1.0, 0.0)
    denom = 1.0 + jnp.dot(
        curv, wide, precision=lax.Precision.HIGHEST, preferred_element_type=jnp.float32
    )
    at = lax.axis_index(NEAR) * RUN
    old = gains_ref[pl.ds(pl.multiple_of(at, RUN), RUN), :]
    return old - STEP * grad / denom, grad / jnp.sqrt(denom)


def step_kernel(parts_ref, gains_ref, copies_ref):
    gains, _ = stepped(parts_ref, gains_ref)
    for at in range(0, copies_ref.shape[0], RUN):
        copies_ref[at : at + RUN, :] = gains


def last_kernel(parts_ref, gains_ref, gains_out_ref, white_ref):
    owned = gains_out_ref.shape[1]
    first = lax.axis_index("z1") * (RUN // 2)
    source = lax.broadcasted_iota(jnp.int32, (RUN, owned), 0) - first
    target = lax.broadcasted_iota(jnp.int32, (RUN, owned), 1)
    results = stepped(parts_ref, gains_ref)
    for value, out_ref in zip(results, (gains_out_ref, white_ref)):
        out = None
        for odd in range(2):
            part = lax.dot_general(
                value[:, odd * VALS : (odd + 1) * VALS],
                jnp.where(target == 2 * source + odd, 1.0, 0.0),
                (((0,), (0,)), ((), ())),
                precision=lax.Precision.HIGHEST,
                preferred_element_type=jnp.float32,
            )
            out = part if out is None else out + part
        out_ref[...] = out


def step(parts, gains, peers):
    return pl.pallas_call(
        step_kernel,
        out_shape=jax.ShapeDtypeStruct((peers * RUN, LANES), jnp.float32),
        in_specs=[pl.BlockSpec(memory_space=pltpu.VMEM)] * 2,
        out_specs=pl.BlockSpec(memory_space=pltpu.VMEM),
        compiler_params=pltpu.CompilerParams(vmem_limit_bytes=16 * 2**20),
        name="step",
    )(parts, gains)


def last(parts, gains, owned):
    return pl.pallas_call(
        last_kernel,
        out_shape=(jax.ShapeDtypeStruct((VALS, owned), jnp.float32),) * 2,
        in_specs=[pl.BlockSpec(memory_space=pltpu.VMEM)] * 2,
        out_specs=tuple([pl.BlockSpec(memory_space=pltpu.VMEM)] * 2),
        compiler_params=pltpu.CompilerParams(vmem_limit_bytes=16 * 2**20),
        name="last",
    )(parts, gains)


def exchange(rows, axes, peers):
    count = rows.shape[0]
    sent = rows.reshape(peers, 1, count // peers * LANES)
    return lax.all_to_all(sent, axes, 0, 0).reshape(count, LANES)


def per_device(model, vis, weights, antenna1, antenna2, live, gains):
    base = antenna1.shape[0]
    channels = model.shape[1]
    owned = gains.shape[3]
    model = model.reshape(channels, VALS, base)
    vis, weights = vis[0], weights[0]
    first, second, live = (a.reshape(1, base) for a in (antenna1, antenna2, live))
    mine = gains.reshape(VALS, owned).T.reshape(1, owned * VALS // LANES, LANES)
    mine = jnp.broadcast_to(mine, (32,) + mine.shape[1:]).reshape(-1, LANES)
    full = exchange(mine, NEAR + ("z1",), 32)
    for turn in range(ITERS):
        sent = partials(full, model, vis, weights, live, first, second)
        sent = total(exchange(sent, NEAR, 16), 16)
        sums = exchange(sent, FAR, 16)
        if turn < ITERS - 1:
            full = exchange(step(sums, full, 16), NEAR, 16)
    return tuple(out.reshape(gains.shape) for out in last(sums, full, owned))


def solution(mesh):
    fine = Mesh(mesh.devices.reshape(8, 4, 2, 2, 2, 2), ("y", "x", "z1", "z0", "core", "chan"))
    bl = ("x", "z1", "z0", "core")
    return jax.shard_map(
        per_device,
        mesh=fine,
        in_specs=(
            P("y", "chan", None, None, bl),
            P("y", "chan", None, bl),
            P("y", "chan", bl),
            P(bl),
            P(bl),
            P(bl),
            P("chan", None, None, bl),
        ),
        out_specs=(P("chan", None, None, bl), P("chan", None, None, bl)),
        check_vma=False,
    )
```

```python
import functools

import jax
import jax.numpy as jnp
from jax import lax
from jax.experimental import pallas as pl
from jax.experimental.pallas import tpu as pltpu
from jax.sharding import Mesh
from jax.sharding import PartitionSpec as P

ITERS = 3
STEP = 0.8
DIRS = 8
COMPS = 8
VALS = DIRS * COMPS
LANES = 128
RUN = LANES // DIRS
NEAR = ("x", "z0", "core")
FAR = ("z1", "y")
WIDE = NEAR + ("z1",)


def cmul(left, right):
    return (left[0] * right[0] - left[1] * right[1], left[0] * right[1] + left[1] * right[0])


def cadd(left, right):
    return (left[0] + right[0], left[1] + right[1])


def adjoint(matrix):
    return [(entry[0], -entry[1]) for entry in (matrix[0], matrix[2], matrix[1], matrix[3])]


def product(left, right):
    result = []
    for row in range(2):
        for col in range(2):
            result.append(
                cadd(cmul(left[2 * row], right[col]), cmul(left[2 * row + 1], right[2 + col]))
            )
    return result


def norm_sq(matrix):
    return sum(entry[0] * entry[0] + entry[1] * entry[1] for entry in matrix)


def halves(value):
    high = value.astype(jnp.bfloat16)
    low = (value - high.astype(jnp.float32)).astype(jnp.bfloat16)
    return high, low


def select_sum(left, right, dims):
    rows = left.shape[0]
    both = lax.dot_general(
        jnp.concatenate(halves(left), axis=0), right, (dims, ((), ())),
        preferred_element_type=jnp.float32,
    )
    return both[:rows] + both[rows:]


def pick_sum(left, right, dims):
    rows = right.shape[0]
    both = lax.dot_general(
        left, jnp.concatenate(halves(right), axis=0), (dims, ((), ())),
        preferred_element_type=jnp.float32,
    )
    return both[:, :rows] + both[:, rows:]


def placed(station):
    kept = station & 0b110001111
    return kept | ((station & 0b110000) << 1) | ((station >> 2) & 0b10000)


def in_vmem(count):
    return [pl.BlockSpec(memory_space=pltpu.VMEM)] * count


PARAMS = pltpu.CompilerParams(vmem_limit_bytes=16 * 2**20)


def pack_kernel(
    model_hbm, vis_hbm, weight_hbm, live_hbm, first_hbm, second_hbm, gains_hbm,
    data_ref, own_ref, copies_ref,
    model_ref, vis_ref, weight_ref, live_ref, first_ref, second_ref, gains_ref, sems,
):
    pairs = (
        (gains_hbm, gains_ref), (model_hbm, model_ref), (vis_hbm, vis_ref), (weight_hbm, weight_ref),
        (live_hbm, live_ref), (first_hbm, first_ref), (second_hbm, second_ref),
    )
    moves = [
        pltpu.make_async_copy(source, target, sems.at[index])
        for index, (source, target) in enumerate(pairs)
    ]
    for move in moves:
        move.start()
    moves[0].wait()
    owned = gains_ref.shape[1]
    target = lax.broadcasted_iota(jnp.int32, (owned // 2, owned), 0)
    source = lax.broadcasted_iota(jnp.int32, (owned // 2, owned), 1)
    mine = jnp.concatenate(
        [
            lax.dot_general(
                jnp.where(source == 2 * target + odd, 1.0, 0.0),
                gains_ref[...],
                (((1,), (1,)), ((), ())),
                precision=lax.Precision.HIGHEST,
                preferred_element_type=jnp.float32,
            )
            for odd in range(2)
        ],
        axis=1,
    )
    for at in range(0, copies_ref.shape[0], owned // 2):
        copies_ref[at : at + owned // 2, :] = mine
    for move in moves[1:]:
        move.wait()

    channels, base = weight_ref.shape
    cuts = base // LANES
    live = live_ref[...].astype(jnp.float32)
    tail = []
    for part in range(channels * cuts):
        channel, cut = divmod(part, cuts)
        lanes = slice(cut * LANES, (cut + 1) * LANES)
        at = part * (VALS + COMPS)
        for ref in (data_ref, own_ref):
            ref[at : at + VALS, :] = model_ref[channel, :, lanes].astype(jnp.float32)
            ref[at + VALS : at + VALS + COMPS, :] = vis_ref[channel, :, lanes]
        tail.append(weight_ref[channel : channel + 1, lanes] * live[:, lanes])
    for station_ref in (first_ref, second_ref):
        station = station_ref[...].astype(jnp.float32)
        tail += [station[:, cut * LANES : (cut + 1) * LANES] for cut in range(cuts)]
    for ref in (data_ref, own_ref):
        ref[channels * cuts * (VALS + COMPS) :, :] = jnp.concatenate(tail, axis=0)


def pack(model, vis, weights, live, first, second, gains, peers):
    channels, base = weights.shape
    cuts = base // LANES
    rows = channels * cuts * (VALS + COMPS + 1) + 2 * cuts
    args = (model, vis, weights, live, first, second, gains)
    return pl.pallas_call(
        pack_kernel,
        out_shape=(
            jax.ShapeDtypeStruct((rows, LANES), jnp.float32),
            jax.ShapeDtypeStruct((rows, LANES), jnp.float32),
            jax.ShapeDtypeStruct((peers * gains.shape[1] // 2, LANES), jnp.float32),
        ),
        in_specs=[pl.BlockSpec(memory_space=pltpu.HBM)] * len(args),
        out_specs=tuple(in_vmem(3)),
        scratch_shapes=[pltpu.VMEM(a.shape, a.dtype) for a in args]
        + [pltpu.SemaphoreType.DMA((len(args),))],
        compiler_params=pltpu.CompilerParams(vmem_limit_bytes=63 * 2**20),
        name="pack",
    )(*args)


def partials_kernel(
    run, channels, gains_ref, data_ref, out_ref, picked_ref, terms_ref
):
    pairs = gains_ref.shape[0]
    times = data_ref.shape[0]
    cuts = picked_ref.shape[0] // 2
    base = cuts * LANES
    tail = channels * cuts * (VALS + COMPS + 1)
    ends = [data_ref[0, tail + end : tail + end + 1, :] for end in range(2 * cuts)]
    station = placed(jnp.concatenate(ends, axis=1).astype(jnp.int32))
    rows = lax.broadcasted_iota(jnp.int32, (pairs, 2 * base), 0)
    hot = jnp.where(rows == station // 2, 1.0, 0.0).astype(jnp.bfloat16)
    odd = station % 2 == 1

    both = select_sum(gains_ref[...].T, hot, ((1,), (0,)))
    picked = jnp.where(odd, both[VALS:], both[:VALS])
    for cut in range(2 * cuts):
        picked_ref[cut] = picked[:, cut * LANES : (cut + 1) * LANES]

    def entries(ref, outer, at):
        comps = [ref[outer, pl.ds(at + c, DIRS, stride=COMPS), :] for c in range(COMPS)]
        return [(comps[i], comps[i + 4]) for i in range(4)]

    curvs = [None] * (2 * cuts)
    for cut in range(cuts):
        near = entries(picked_ref, cut, 0)
        far = entries(picked_ref, cuts + cut, 0)

        def at_time(time, totals, cut=cut, near=near, far=far):
            for channel in range(channels):
                part = channel * cuts + cut
                at = part * (VALS + COMPS)
                model = entries(data_ref, time, at)
                vis = data_ref[time, at + VALS : at + VALS + COMPS, :]
                row = channels * cuts * (VALS + COMPS) + part
                scale = data_ref[time, row : row + 1, :]
                right_a = product(model, adjoint(far))
                left_b = product(near, model)
                each = product(near, right_a)
                resid = []
                for index in range(4):
                    pred_re = jnp.sum(each[index][0], axis=0, keepdims=True)
                    pred_im = jnp.sum(each[index][1], axis=0, keepdims=True)
                    resid.append(
                        (
                            scale * (vis[index : index + 1] - pred_re),
                            scale * (vis[index + 4 : index + 5] - pred_im),
                        )
                    )
                new = (
                    product(resid, adjoint(right_a)),
                    product(adjoint(resid), left_b),
                    scale * norm_sq(right_a),
                    scale * norm_sq(left_b),
                )
                totals = new if totals is None else jax.tree.map(jnp.add, totals, new)
            return totals

        totals = at_time(0, None)
        for time in range(1, times):
            totals = at_time(time, totals)
        for side in range(2):
            at = side * cuts + cut
            for index, (real, imag) in enumerate(totals[side]):
                terms_ref[at, pl.ds(index, DIRS, stride=COMPS), :] = -real
                terms_ref[at, pl.ds(index + 4, DIRS, stride=COMPS), :] = -imag
            curvs[at] = totals[2 + side]

    terms = jnp.concatenate([terms_ref[at] for at in range(2 * cuts)], axis=1)
    curv = jnp.concatenate(curvs, axis=1)
    spread = jnp.concatenate([jnp.where(odd, 0.0, terms), jnp.where(odd, terms, 0.0)], axis=0)
    grads = pick_sum(hot, spread, ((1,), (1,)))
    wide = jnp.concatenate([curv] * RUN, axis=0)
    seat = lax.broadcasted_iota(jnp.int32, wide.shape, 0) // DIRS
    spread = jnp.where(seat == station % RUN, wide, 0.0)
    rows = lax.broadcasted_iota(jnp.int32, (2 * pairs // RUN, 2 * base), 0)
    hot = jnp.where(rows == station // RUN, 1.0, 0.0).astype(jnp.bfloat16)
    curvs = pick_sum(hot, spread, ((1,), (1,)))
    extra = run // 8
    for peer in range(pairs // run):
        at = peer * (run + extra)
        out_ref[at : at + run, :] = grads[peer * run : (peer + 1) * run]
        out_ref[at + run : at + run + extra, :] = curvs[peer * extra : (peer + 1) * extra]


def partials(run, channels, gains, data):
    pairs = gains.shape[0]
    cuts = data.shape[1] // (channels * (VALS + COMPS + 1) + 2)
    return pl.pallas_call(
        functools.partial(partials_kernel, run, channels),
        out_shape=jax.ShapeDtypeStruct((pairs // 8 * 9, LANES), jnp.float32),
        in_specs=in_vmem(2),
        out_specs=in_vmem(1)[0],
        scratch_shapes=[pltpu.VMEM((2 * cuts, VALS, LANES), jnp.float32)] * 2,
        compiler_params=PARAMS,
        name="partials",
    )(gains, data)


def peers_sum(parts_ref, rows):
    total = parts_ref[0:rows, :]
    for at in range(rows, parts_ref.shape[0], rows):
        total = total + parts_ref[at : at + rows, :]
    return total


def total_kernel(rows, parts_ref, copies_ref):
    total = peers_sum(parts_ref, rows)
    for at in range(0, copies_ref.shape[0], rows):
        copies_ref[at : at + rows, :] = total


def total(run, parts, peers):
    rows = run // 8 * 9
    return pl.pallas_call(
        functools.partial(total_kernel, rows),
        out_shape=jax.ShapeDtypeStruct((peers * rows, LANES), jnp.float32),
        in_specs=in_vmem(1),
        out_specs=in_vmem(1)[0],
        compiler_params=PARAMS,
        name="total",
    )(parts)


def stepped(run, parts_ref, gains_ref):
    sums = peers_sum(parts_ref, run // 8 * 9)
    grad = sums[:run]
    row = lax.broadcasted_iota(jnp.int32, (run, LANES), 0)
    lane = lax.broadcasted_iota(jnp.int32, (run, LANES), 1)
    curv = sums[run : run + 1]
    for extra in range(1, run // 8):
        curv = jnp.where(row < 8 * extra, curv, sums[run + extra : run + extra + 1])
    curv = jnp.where(lane // (2 * DIRS) == row % 8, curv, 0.0)
    source = lax.broadcasted_iota(jnp.int32, (LANES, LANES), 0)
    target = lax.broadcasted_iota(jnp.int32, (LANES, LANES), 1)
    wide = jnp.where(source % (2 * DIRS) == target // COMPS, 1.0, 0.0)
    denom = 1.0 + jnp.dot(
        curv, wide, precision=lax.Precision.HIGHEST, preferred_element_type=jnp.float32
    )
    at = lax.axis_index(NEAR if run == RUN else WIDE) * run
    old = gains_ref[pl.ds(pl.multiple_of(at, run), run), :]
    return old - STEP * grad / denom, grad / jnp.sqrt(denom)


def step_kernel(run, parts_ref, gains_ref, copies_ref):
    gains, _ = stepped(run, parts_ref, gains_ref)
    for at in range(0, copies_ref.shape[0], run):
        copies_ref[at : at + run, :] = gains


def last_kernel(run, parts_ref, gains_ref, gains_out_ref, white_ref):
    owned = 2 * run
    source = lax.broadcasted_iota(jnp.int32, (run, owned), 0)
    target = lax.broadcasted_iota(jnp.int32, (run, owned), 1)
    results = stepped(run, parts_ref, gains_ref)
    for value, out_ref in zip(results, (gains_out_ref, white_ref)):
        out = None
        for odd in range(2):
            part = lax.dot_general(
                value[:, odd * VALS : (odd + 1) * VALS],
                jnp.where(target == 2 * source + odd, 1.0, 0.0),
                (((0,), (0,)), ((), ())),
                precision=lax.Precision.HIGHEST,
                preferred_element_type=jnp.float32,
            )
            out = part if out is None else out + part
        out_ref[...] = out


def step(run, parts, gains):
    return pl.pallas_call(
        functools.partial(step_kernel, run),
        out_shape=jax.ShapeDtypeStruct(gains.shape, jnp.float32),
        in_specs=in_vmem(2),
        out_specs=in_vmem(1)[0],
        compiler_params=PARAMS,
        name="step",
    )(parts, gains)


def last(run, parts, gains):
    return pl.pallas_call(
        functools.partial(last_kernel, run),
        out_shape=(jax.ShapeDtypeStruct((VALS, 2 * run), jnp.float32),) * 2,
        in_specs=in_vmem(2),
        out_specs=tuple(in_vmem(2)),
        compiler_params=PARAMS,
        name="last",
    )(parts, gains)


def exchange(rows, axes, peers):
    count = rows.shape[0]
    sent = rows.reshape(peers, 1, count // peers * LANES)
    return lax.all_to_all(sent, axes, 0, 0).reshape(count, LANES)


def per_device(model, vis, weights, antenna1, antenna2, live, gains):
    base = antenna1.shape[0]
    channels = model.shape[1]
    first, second, live = (a.reshape(1, base) for a in (antenna1, antenna2, live))
    data, own, copies = pack(
        model.reshape(channels, VALS, base), vis[0], weights[0], live, first, second,
        gains.reshape(VALS, gains.shape[3]), 32,
    )
    every = lax.all_gather(data, "y")
    full = exchange(copies, WIDE, 32)
    parts = exchange(partials(RUN, channels, full, own[None]), NEAR, 16)
    sums = exchange(total(RUN, parts, 16), FAR, 16)
    full = exchange(step(RUN, sums, full), NEAR, 16)
    for turn in range(1, ITERS):
        sums = exchange(partials(RUN // 2, channels, full, every), WIDE, 32)
        if turn < ITERS - 1:
            full = exchange(step(RUN // 2, sums, full), WIDE, 32)
    return tuple(out.reshape(gains.shape) for out in last(RUN // 2, sums, full))


def solution(mesh):
    fine = Mesh(mesh.devices.reshape(8, 4, 2, 2, 2, 2), ("y", "x", "z1", "z0", "core", "chan"))
    bl = ("x", "z1", "z0", "core")
    return jax.shard_map(
        per_device,
        mesh=fine,
        in_specs=(
            P("y", "chan", None, None, bl),
            P("y", "chan", None, bl),
            P("y", "chan", bl),
            P(bl),
            P(bl),
            P(bl),
            P("chan", None, None, bl),
        ),
        out_specs=(P("chan", None, None, bl), P("chan", None, None, bl)),
        check_vma=False,
    )
```

```python
import functools

import jax
import jax.numpy as jnp
from jax import lax
from jax.experimental import pallas as pl
from jax.experimental.pallas import tpu as pltpu
from jax.sharding import Mesh
from jax.sharding import PartitionSpec as P

ITERS = 3
STEP = 0.8
DIRS = 8
COMPS = 8
VALS = DIRS * COMPS
LANES = 128
RUN = LANES // DIRS
NEAR = ("x", "z0", "core")
FAR = ("z1", "y")


def cmul(left, right):
    return (left[0] * right[0] - left[1] * right[1], left[0] * right[1] + left[1] * right[0])


def cadd(left, right):
    return (left[0] + right[0], left[1] + right[1])


def adjoint(matrix):
    return [(entry[0], -entry[1]) for entry in (matrix[0], matrix[2], matrix[1], matrix[3])]


def product(left, right):
    result = []
    for row in range(2):
        for col in range(2):
            result.append(
                cadd(cmul(left[2 * row], right[col]), cmul(left[2 * row + 1], right[2 + col]))
            )
    return result


def norm_sq(matrix):
    return sum(entry[0] * entry[0] + entry[1] * entry[1] for entry in matrix)


def halves(value):
    high = value.astype(jnp.bfloat16)
    low = (value - high.astype(jnp.float32)).astype(jnp.bfloat16)
    return high, low


def select_sum(left, right, dims):
    rows = left.shape[0]
    both = lax.dot_general(
        jnp.concatenate(halves(left), axis=0), right, (dims, ((), ())),
        preferred_element_type=jnp.float32,
    )
    return both[:rows] + both[rows:]


def pick_sum(left, right, dims):
    rows = right.shape[0]
    both = lax.dot_general(
        left, jnp.concatenate(halves(right), axis=0), (dims, ((), ())),
        preferred_element_type=jnp.float32,
    )
    return both[:, :rows] + both[:, rows:]


def placed(station):
    kept = station & 0b110001111
    return kept | ((station & 0b110000) << 1) | ((station >> 2) & 0b10000)


def partials_kernel(
    gains_ref, model_ref, vis_ref, weight_ref, live_ref, first_ref, second_ref,
    out_ref, picked_ref, model_f_ref, terms_ref,
):
    base = first_ref.shape[1]
    pairs = gains_ref.shape[0]
    channels = model_ref.shape[0]
    station = placed(jnp.concatenate([first_ref[...], second_ref[...]], axis=1))
    rows = lax.broadcasted_iota(jnp.int32, (pairs, 2 * base), 0)
    hot = jnp.where(rows == station // 2, 1.0, 0.0).astype(jnp.bfloat16)
    odd = station % 2 == 1

    both = select_sum(gains_ref[...].T, hot, ((1,), (0,)))
    picked = jnp.where(odd, both[VALS:], both[:VALS])
    cuts = base // LANES
    for cut in range(2 * cuts):
        picked_ref[cut] = picked[:, cut * LANES : (cut + 1) * LANES]

    def entries(ref, at):
        comps = [ref[at, pl.ds(c, DIRS, stride=COMPS), :] for c in range(COMPS)]
        return [(comps[i], comps[i + 4]) for i in range(4)]

    live = live_ref[...].astype(jnp.float32)
    curvs = [None] * (2 * cuts)
    for cut in range(cuts):
        lanes = slice(cut * LANES, (cut + 1) * LANES)
        near = entries(picked_ref, cut)
        far = entries(picked_ref, cuts + cut)
        totals = None
        for channel in range(channels):
            model_f_ref[0] = model_ref[channel, :, lanes].astype(jnp.float32)
            model = entries(model_f_ref, 0)
            scale = weight_ref[channel : channel + 1, lanes] * live[:, lanes]
            right_a = product(model, adjoint(far))
            left_b = product(near, model)
            each = product(near, right_a)
            vis = vis_ref[channel, :, lanes]
            resid = []
            for index in range(4):
                pred_re = jnp.sum(each[index][0], axis=0, keepdims=True)
                pred_im = jnp.sum(each[index][1], axis=0, keepdims=True)
                resid.append(
                    (
                        scale * (vis[index : index + 1] - pred_re),
                        scale * (vis[index + 4 : index + 5] - pred_im),
                    )
                )
            new = (
                product(resid, adjoint(right_a)),
                product(adjoint(resid), left_b),
                scale * norm_sq(right_a),
                scale * norm_sq(left_b),
            )
            totals = new if totals is None else jax.tree.map(lambda a, b: a + b, totals, new)
        for side in range(2):
            at = side * cuts + cut
            for index, (real, imag) in enumerate(totals[side]):
                terms_ref[at, pl.ds(index, DIRS, stride=COMPS), :] = -real
                terms_ref[at, pl.ds(index + 4, DIRS, stride=COMPS), :] = -imag
            curvs[at] = totals[2 + side]

    terms = jnp.concatenate([terms_ref[at] for at in range(2 * cuts)], axis=1)
    curv = jnp.concatenate(curvs, axis=1)
    spread = jnp.concatenate([jnp.where(odd, 0.0, terms), jnp.where(odd, terms, 0.0)], axis=0)
    grads = pick_sum(hot, spread, ((1,), (1,)))
    wide = jnp.concatenate([curv] * RUN, axis=0)
    seat = lax.broadcasted_iota(jnp.int32, wide.shape, 0) // DIRS
    spread = jnp.where(seat == station % RUN, wide, 0.0)
    rows = lax.broadcasted_iota(jnp.int32, (2 * pairs // RUN, 2 * base), 0)
    hot = jnp.where(rows == station // RUN, 1.0, 0.0).astype(jnp.bfloat16)
    curvs = pick_sum(hot, spread, ((1,), (1,)))
    for peer in range(pairs // RUN):
        at = peer * (RUN + 2)
        out_ref[at : at + RUN, :] = grads[peer * RUN : (peer + 1) * RUN]
        out_ref[at + RUN : at + RUN + 2, :] = curvs[2 * peer : 2 * peer + 2]


def partials(gains, model, vis, weights, live, first, second):
    pairs = gains.shape[0]
    base = first.shape[1]
    return pl.pallas_call(
        partials_kernel,
        out_shape=jax.ShapeDtypeStruct((pairs // RUN * (RUN + 2), LANES), jnp.float32),
        in_specs=[pl.BlockSpec(memory_space=pltpu.VMEM)] * 7,
        out_specs=pl.BlockSpec(memory_space=pltpu.VMEM),
        scratch_shapes=[
            pltpu.VMEM((2 * base // LANES, VALS, LANES), jnp.float32),
            pltpu.VMEM((1, VALS, LANES), jnp.float32),
            pltpu.VMEM((2 * base // LANES, VALS, LANES), jnp.float32),
        ],
        compiler_params=pltpu.CompilerParams(vmem_limit_bytes=16 * 2**20),
        name="partials",
    )(gains, model, vis, weights, live, first, second)


def peers_sum(parts_ref, rows):
    total = parts_ref[0:rows, :]
    for at in range(rows, parts_ref.shape[0], rows):
        total = total + parts_ref[at : at + rows, :]
    return total


def total_kernel(parts_ref, copies_ref):
    total = peers_sum(parts_ref, RUN + 2)
    for at in range(0, copies_ref.shape[0], RUN + 2):
        copies_ref[at : at + RUN + 2, :] = total


def total_halves_kernel(parts_ref, copies_ref):
    total = peers_sum(parts_ref, RUN + 2)
    run = RUN // 2
    count = copies_ref.shape[0] // 2
    for half in range(2):
        own = jnp.concatenate(
            [total[half * run : (half + 1) * run], total[RUN + half : RUN + half + 1]], axis=0
        )
        for at in range(half * count, (half + 1) * count, run + 1):
            copies_ref[at : at + run + 1, :] = own


def total(parts, peers, kernel, rows):
    return pl.pallas_call(
        kernel,
        out_shape=jax.ShapeDtypeStruct((peers * rows, LANES), jnp.float32),
        in_specs=[pl.BlockSpec(memory_space=pltpu.VMEM)],
        out_specs=pl.BlockSpec(memory_space=pltpu.VMEM),
        compiler_params=pltpu.CompilerParams(vmem_limit_bytes=16 * 2**20),
        name="total",
    )(parts)


def stepped(run, at, parts_ref, gains_ref):
    sums = peers_sum(parts_ref, run // 8 * 9)
    grad = sums[:run]
    row = lax.broadcasted_iota(jnp.int32, (run, LANES), 0)
    lane = lax.broadcasted_iota(jnp.int32, (run, LANES), 1)
    curv = sums[run : run + 1]
    if run > 8:
        curv = jnp.where(row < 8, curv, sums[run + 1 : run + 2])
    curv = jnp.where(lane // (2 * DIRS) == row % 8, curv, 0.0)
    source = lax.broadcasted_iota(jnp.int32, (LANES, LANES), 0)
    target = lax.broadcasted_iota(jnp.int32, (LANES, LANES), 1)
    wide = jnp.where(source % (2 * DIRS) == target // COMPS, 1.0, 0.0)
    denom = 1.0 + jnp.dot(
        curv, wide, precision=lax.Precision.HIGHEST, preferred_element_type=jnp.float32
    )
    old = gains_ref[pl.ds(pl.multiple_of(at, run), run), :]
    return old - STEP * grad / denom, grad / jnp.sqrt(denom)


def step_kernel(parts_ref, gains_ref, copies_ref):
    gains, _ = stepped(RUN, lax.axis_index(NEAR) * RUN, parts_ref, gains_ref)
    for at in range(0, copies_ref.shape[0], RUN):
        copies_ref[at : at + RUN, :] = gains


def last_kernel(parts_ref, gains_ref, gains_out_ref, white_ref):
    owned = gains_out_ref.shape[1]
    run = RUN // 2
    at = lax.axis_index(NEAR) * RUN + lax.axis_index("z1") * run
    source = lax.broadcasted_iota(jnp.int32, (run, owned), 0)
    target = lax.broadcasted_iota(jnp.int32, (run, owned), 1)
    results = stepped(run, at, parts_ref, gains_ref)
    for value, out_ref in zip(results, (gains_out_ref, white_ref)):
        out = None
        for odd in range(2):
            part = lax.dot_general(
                value[:, odd * VALS : (odd + 1) * VALS],
                jnp.where(target == 2 * source + odd, 1.0, 0.0),
                (((0,), (0,)), ((), ())),
                precision=lax.Precision.HIGHEST,
                preferred_element_type=jnp.float32,
            )
            out = part if out is None else out + part
        out_ref[...] = out


def step(parts, gains, peers):
    return pl.pallas_call(
        step_kernel,
        out_shape=jax.ShapeDtypeStruct((peers * RUN, LANES), jnp.float32),
        in_specs=[pl.BlockSpec(memory_space=pltpu.VMEM)] * 2,
        out_specs=pl.BlockSpec(memory_space=pltpu.VMEM),
        compiler_params=pltpu.CompilerParams(vmem_limit_bytes=16 * 2**20),
        name="step",
    )(parts, gains)


def last(parts, gains, owned):
    return pl.pallas_call(
        last_kernel,
        out_shape=(jax.ShapeDtypeStruct((VALS, owned), jnp.float32),) * 2,
        in_specs=[pl.BlockSpec(memory_space=pltpu.VMEM)] * 2,
        out_specs=(pl.BlockSpec(memory_space=pltpu.VMEM),) * 2,
        compiler_params=pltpu.CompilerParams(vmem_limit_bytes=16 * 2**20),
        name="last",
    )(parts, gains)


def exchange(rows, axes, peers):
    count = rows.shape[0]
    sent = rows.reshape(peers, 1, count // peers * LANES)
    return lax.all_to_all(sent, axes, 0, 0).reshape(count, LANES)


def per_device(model, vis, weights, antenna1, antenna2, live, gains):
    base = antenna1.shape[0]
    channels = model.shape[1]
    owned = gains.shape[3]
    model = model.reshape(channels, VALS, base)
    vis, weights = vis[0], weights[0]
    first, second, live = (a.reshape(1, base) for a in (antenna1, antenna2, live))
    mine = gains.reshape(VALS, owned).T.reshape(1, owned * VALS // LANES, LANES)
    mine = jnp.broadcast_to(mine, (32,) + mine.shape[1:]).reshape(-1, LANES)
    full = exchange(mine, NEAR + ("z1",), 32)
    for turn in range(ITERS):
        sent = partials(full, model, vis, weights, live, first, second)
        parts = exchange(sent, NEAR, 16)
        if turn < ITERS - 1:
            sums = exchange(total(parts, 16, total_kernel, RUN + 2), FAR, 16)
            full = exchange(step(sums, full, 16), NEAR, 16)
        else:
            sums = exchange(total(parts, 16, total_halves_kernel, RUN // 2 + 1), FAR, 16)
    return tuple(out.reshape(gains.shape) for out in last(sums, full, owned))


def solution(mesh):
    fine = Mesh(mesh.devices.reshape(8, 4, 2, 2, 2, 2), ("y", "x", "z1", "z0", "core", "chan"))
    bl = ("x", "z1", "z0", "core")
    return jax.shard_map(
        per_device,
        mesh=fine,
        in_specs=(
            P("y", "chan", None, None, bl),
            P("y", "chan", None, bl),
            P("y", "chan", bl),
            P(bl),
            P(bl),
            P(bl),
            P("chan", None, None, bl),
        ),
        out_specs=(P("chan", None, None, bl), P("chan", None, None, bl)),
        check_vma=False,
    )
```

```python
import functools

import jax
import jax.numpy as jnp
from jax import lax
from jax.experimental import pallas as pl
from jax.experimental.pallas import tpu as pltpu
from jax.sharding import Mesh
from jax.sharding import PartitionSpec as P

ITERS = 3
STEP = 0.8
DIRS = 8
COMPS = 8
VALS = DIRS * COMPS
LANES = 128
RUN = LANES // DIRS
NEAR = ("x", "z0", "core")
FAR = ("z1", "y")


def cmul(left, right):
    return (left[0] * right[0] - left[1] * right[1], left[0] * right[1] + left[1] * right[0])


def cadd(left, right):
    return (left[0] + right[0], left[1] + right[1])


def adjoint(matrix):
    return [(entry[0], -entry[1]) for entry in (matrix[0], matrix[2], matrix[1], matrix[3])]


def product(left, right):
    result = []
    for row in range(2):
        for col in range(2):
            result.append(
                cadd(cmul(left[2 * row], right[col]), cmul(left[2 * row + 1], right[2 + col]))
            )
    return result


def norm_sq(matrix):
    return sum(entry[0] * entry[0] + entry[1] * entry[1] for entry in matrix)


def halves(value):
    high = value.astype(jnp.bfloat16)
    low = (value - high.astype(jnp.float32)).astype(jnp.bfloat16)
    return high, low


def select_sum(left, right, dims):
    rows = left.shape[0]
    both = lax.dot_general(
        jnp.concatenate(halves(left), axis=0), right, (dims, ((), ())),
        preferred_element_type=jnp.float32,
    )
    return both[:rows] + both[rows:]


def pick_sum(left, right, dims):
    rows = right.shape[0]
    both = lax.dot_general(
        left, jnp.concatenate(halves(right), axis=0), (dims, ((), ())),
        preferred_element_type=jnp.float32,
    )
    return both[:, :rows] + both[:, rows:]


def placed(station):
    kept = station & 0b110001111
    return kept | ((station & 0b110000) << 1) | ((station >> 2) & 0b10000)


def open_kernel(*refs):
    sources, (copies_ref, rows_ref), targets, sems = refs[:5], refs[5:7], refs[7:12], refs[12]
    moves = [
        pltpu.make_async_copy(source, target, sems.at[index])
        for index, (source, target) in enumerate(zip(sources, targets))
    ]
    for move in moves:
        move.start()
    for move in moves:
        move.wait()
    gains_ref, weight_ref, live_ref, first_ref, second_ref = targets
    owned = gains_ref.shape[1]
    target = lax.broadcasted_iota(jnp.int32, (owned // 2, owned), 0)
    source = lax.broadcasted_iota(jnp.int32, (owned // 2, owned), 1)
    mine = jnp.concatenate(
        [
            lax.dot_general(
                jnp.where(source == 2 * target + odd, 1.0, 0.0),
                gains_ref[...],
                (((1,), (1,)), ((), ())),
                precision=lax.Precision.HIGHEST,
                preferred_element_type=jnp.float32,
            )
            for odd in range(2)
        ],
        axis=1,
    )
    for at in range(0, copies_ref.shape[0], owned // 2):
        copies_ref[at : at + owned // 2, :] = mine
    live = live_ref[...].astype(jnp.float32)
    lines = [weight_ref[c : c + 1, :] * live for c in range(weight_ref.shape[0])]
    lines += [first_ref[...].astype(jnp.float32), second_ref[...].astype(jnp.float32)]
    cuts = live.shape[1] // LANES
    rows_ref[...] = jnp.concatenate(
        [line[:, cut * LANES : (cut + 1) * LANES] for line in lines for cut in range(cuts)], axis=0
    )


def opened(peers, *args):
    gains, weights = args[:2]
    channels, base = weights.shape
    return pl.pallas_call(
        open_kernel,
        out_shape=(
            jax.ShapeDtypeStruct((peers * gains.shape[1] // 2, LANES), jnp.float32),
            jax.ShapeDtypeStruct(((channels + 2) * base // LANES, LANES), jnp.float32),
        ),
        in_specs=[pl.BlockSpec(memory_space=pltpu.HBM)] * 5,
        out_specs=(pl.BlockSpec(memory_space=pltpu.VMEM),) * 2,
        scratch_shapes=[pltpu.VMEM(a.shape, a.dtype) for a in args]
        + [pltpu.SemaphoreType.DMA((5,))],
        compiler_params=pltpu.CompilerParams(vmem_limit_bytes=16 * 2**20),
        name="opened",
    )(*(pltpu.with_memory_space_constraint(a, pltpu.HBM) for a in args))


def partials_kernel(
    gains_ref, model_ref, vis_ref, rows_ref, out_ref, picked_ref, model_f_ref, terms_ref
):
    pairs = gains_ref.shape[0]
    channels, _, base = model_ref.shape
    cuts = base // LANES
    ends = [rows_ref[channels * cuts + i : channels * cuts + i + 1, :] for i in range(2 * cuts)]
    station = placed(jnp.concatenate(ends, axis=1).astype(jnp.int32))
    rows = lax.broadcasted_iota(jnp.int32, (pairs, 2 * base), 0)
    hot = jnp.where(rows == station // 2, 1.0, 0.0).astype(jnp.bfloat16)
    odd = station % 2 == 1

    both = select_sum(gains_ref[...].T, hot, ((1,), (0,)))
    picked = jnp.where(odd, both[VALS:], both[:VALS])
    for cut in range(2 * cuts):
        picked_ref[cut] = picked[:, cut * LANES : (cut + 1) * LANES]

    def entries(ref, at):
        comps = [ref[at, pl.ds(c, DIRS, stride=COMPS), :] for c in range(COMPS)]
        return [(comps[i], comps[i + 4]) for i in range(4)]

    curvs = [None] * (2 * cuts)
    for cut in range(cuts):
        lanes = slice(cut * LANES, (cut + 1) * LANES)
        near = entries(picked_ref, cut)
        far = entries(picked_ref, cuts + cut)
        totals = None
        for channel in range(channels):
            model_f_ref[0] = model_ref[channel, :, lanes].astype(jnp.float32)
            model = entries(model_f_ref, 0)
            part = channel * cuts + cut
            scale = rows_ref[part : part + 1, :]
            right_a = product(model, adjoint(far))
            left_b = product(near, model)
            each = product(near, right_a)
            vis = vis_ref[channel, :, lanes]
            resid = []
            for index in range(4):
                pred_re = jnp.sum(each[index][0], axis=0, keepdims=True)
                pred_im = jnp.sum(each[index][1], axis=0, keepdims=True)
                resid.append(
                    (
                        scale * (vis[index : index + 1] - pred_re),
                        scale * (vis[index + 4 : index + 5] - pred_im),
                    )
                )
            new = (
                product(resid, adjoint(right_a)),
                product(adjoint(resid), left_b),
                scale * norm_sq(right_a),
                scale * norm_sq(left_b),
            )
            totals = new if totals is None else jax.tree.map(lambda a, b: a + b, totals, new)
        for side in range(2):
            at = side * cuts + cut
            for index, (real, imag) in enumerate(totals[side]):
                terms_ref[at, pl.ds(index, DIRS, stride=COMPS), :] = -real
                terms_ref[at, pl.ds(index + 4, DIRS, stride=COMPS), :] = -imag
            curvs[at] = totals[2 + side]

    terms = jnp.concatenate([terms_ref[at] for at in range(2 * cuts)], axis=1)
    curv = jnp.concatenate(curvs, axis=1)
    spread = jnp.concatenate([jnp.where(odd, 0.0, terms), jnp.where(odd, terms, 0.0)], axis=0)
    grads = pick_sum(hot, spread, ((1,), (1,)))
    wide = jnp.concatenate([curv] * RUN, axis=0)
    seat = lax.broadcasted_iota(jnp.int32, wide.shape, 0) // DIRS
    spread = jnp.where(seat == station % RUN, wide, 0.0)
    rows = lax.broadcasted_iota(jnp.int32, (2 * pairs // RUN, 2 * base), 0)
    hot = jnp.where(rows == station // RUN, 1.0, 0.0).astype(jnp.bfloat16)
    curvs = pick_sum(hot, spread, ((1,), (1,)))
    for peer in range(pairs // RUN):
        at = peer * (RUN + 2)
        out_ref[at : at + RUN, :] = grads[peer * RUN : (peer + 1) * RUN]
        out_ref[at + RUN : at + RUN + 2, :] = curvs[2 * peer : 2 * peer + 2]


def partials(gains, model, vis, rows):
    pairs = gains.shape[0]
    base = model.shape[2]
    return pl.pallas_call(
        partials_kernel,
        out_shape=jax.ShapeDtypeStruct((pairs // RUN * (RUN + 2), LANES), jnp.float32),
        in_specs=[pl.BlockSpec(memory_space=pltpu.VMEM)] * 4,
        out_specs=pl.BlockSpec(memory_space=pltpu.VMEM),
        scratch_shapes=[
            pltpu.VMEM((2 * base // LANES, VALS, LANES), jnp.float32),
            pltpu.VMEM((1, VALS, LANES), jnp.float32),
            pltpu.VMEM((2 * base // LANES, VALS, LANES), jnp.float32),
        ],
        compiler_params=pltpu.CompilerParams(vmem_limit_bytes=16 * 2**20),
        name="partials",
    )(gains, model, vis, rows)


def peers_sum(parts_ref, rows):
    total = parts_ref[0:rows, :]
    for at in range(rows, parts_ref.shape[0], rows):
        total = total + parts_ref[at : at + rows, :]
    return total


def total_kernel(parts_ref, copies_ref):
    total = peers_sum(parts_ref, RUN + 2)
    for at in range(0, copies_ref.shape[0], RUN + 2):
        copies_ref[at : at + RUN + 2, :] = total


def total_halves_kernel(parts_ref, copies_ref):
    total = peers_sum(parts_ref, RUN + 2)
    run = RUN // 2
    count = copies_ref.shape[0] // 2
    for half in range(2):
        own = jnp.concatenate(
            [total[half * run : (half + 1) * run], total[RUN + half : RUN + half + 1]], axis=0
        )
        for at in range(half * count, (half + 1) * count, run + 1):
            copies_ref[at : at + run + 1, :] = own


def total(parts, peers, kernel, rows):
    return pl.pallas_call(
        kernel,
        out_shape=jax.ShapeDtypeStruct((peers * rows, LANES), jnp.float32),
        in_specs=[pl.BlockSpec(memory_space=pltpu.VMEM)],
        out_specs=pl.BlockSpec(memory_space=pltpu.VMEM),
        compiler_params=pltpu.CompilerParams(vmem_limit_bytes=16 * 2**20),
        name="total",
    )(parts)


def stepped(run, at, parts_ref, gains_ref):
    sums = peers_sum(parts_ref, run // 8 * 9)
    grad = sums[:run]
    row = lax.broadcasted_iota(jnp.int32, (run, LANES), 0)
    lane = lax.broadcasted_iota(jnp.int32, (run, LANES), 1)
    curv = sums[run : run + 1]
    if run > 8:
        curv = jnp.where(row < 8, curv, sums[run + 1 : run + 2])
    curv = jnp.where(lane // (2 * DIRS) == row % 8, curv, 0.0)
    source = lax.broadcasted_iota(jnp.int32, (LANES, LANES), 0)
    target = lax.broadcasted_iota(jnp.int32, (LANES, LANES), 1)
    wide = jnp.where(source % (2 * DIRS) == target // COMPS, 1.0, 0.0)
    denom = 1.0 + jnp.dot(
        curv, wide, precision=lax.Precision.HIGHEST, preferred_element_type=jnp.float32
    )
    old = gains_ref[pl.ds(pl.multiple_of(at, run), run), :]
    return old - STEP * grad / denom, grad / jnp.sqrt(denom)


def step_kernel(parts_ref, gains_ref, copies_ref):
    gains, _ = stepped(RUN, lax.axis_index(NEAR) * RUN, parts_ref, gains_ref)
    for at in range(0, copies_ref.shape[0], RUN):
        copies_ref[at : at + RUN, :] = gains


def last_kernel(parts_ref, gains_ref, gains_out_ref, white_ref):
    owned = gains_out_ref.shape[1]
    run = RUN // 2
    at = lax.axis_index(NEAR) * RUN + lax.axis_index("z1") * run
    source = lax.broadcasted_iota(jnp.int32, (run, owned), 0)
    target = lax.broadcasted_iota(jnp.int32, (run, owned), 1)
    results = stepped(run, at, parts_ref, gains_ref)
    for value, out_ref in zip(results, (gains_out_ref, white_ref)):
        out = None
        for odd in range(2):
            part = lax.dot_general(
                value[:, odd * VALS : (odd + 1) * VALS],
                jnp.where(target == 2 * source + odd, 1.0, 0.0),
                (((0,), (0,)), ((), ())),
                precision=lax.Precision.HIGHEST,
                preferred_element_type=jnp.float32,
            )
            out = part if out is None else out + part
        out_ref[...] = out


def step(parts, gains, peers):
    return pl.pallas_call(
        step_kernel,
        out_shape=jax.ShapeDtypeStruct((peers * RUN, LANES), jnp.float32),
        in_specs=[pl.BlockSpec(memory_space=pltpu.VMEM)] * 2,
        out_specs=pl.BlockSpec(memory_space=pltpu.VMEM),
        compiler_params=pltpu.CompilerParams(vmem_limit_bytes=16 * 2**20),
        name="step",
    )(parts, gains)


def last(parts, gains, owned):
    return pl.pallas_call(
        last_kernel,
        out_shape=(jax.ShapeDtypeStruct((VALS, owned), jnp.float32),) * 2,
        in_specs=[pl.BlockSpec(memory_space=pltpu.VMEM)] * 2,
        out_specs=(pl.BlockSpec(memory_space=pltpu.VMEM),) * 2,
        compiler_params=pltpu.CompilerParams(vmem_limit_bytes=16 * 2**20),
        name="last",
    )(parts, gains)


def exchange(rows, axes, peers):
    count = rows.shape[0]
    sent = rows.reshape(peers, 1, count // peers * LANES)
    return lax.all_to_all(sent, axes, 0, 0).reshape(count, LANES)


def per_device(model, vis, weights, antenna1, antenna2, live, gains):
    base = antenna1.shape[0]
    channels = model.shape[1]
    owned = gains.shape[3]
    model = model.reshape(channels, VALS, base)
    vis, weights = vis[0], weights[0]
    first, second, live = (a.reshape(1, base) for a in (antenna1, antenna2, live))
    copies, rows = opened(32, gains.reshape(VALS, owned), weights, live, first, second)
    full = exchange(copies, NEAR + ("z1",), 32)
    for turn in range(ITERS):
        sent = partials(full, model, vis, rows)
        parts = exchange(sent, NEAR, 16)
        if turn < ITERS - 1:
            sums = exchange(total(parts, 16, total_kernel, RUN + 2), FAR, 16)
            full = exchange(step(sums, full, 16), NEAR, 16)
        else:
            sums = exchange(total(parts, 16, total_halves_kernel, RUN // 2 + 1), FAR, 16)
    return tuple(out.reshape(gains.shape) for out in last(sums, full, owned))


def solution(mesh):
    fine = Mesh(mesh.devices.reshape(8, 4, 2, 2, 2, 2), ("y", "x", "z1", "z0", "core", "chan"))
    bl = ("x", "z1", "z0", "core")
    return jax.shard_map(
        per_device,
        mesh=fine,
        in_specs=(
            P("y", "chan", None, None, bl),
            P("y", "chan", None, bl),
            P("y", "chan", bl),
            P(bl),
            P(bl),
            P(bl),
            P("chan", None, None, bl),
        ),
        out_specs=(P("chan", None, None, bl), P("chan", None, None, bl)),
        check_vma=False,
    )
```

```python
import functools

import jax
import jax.numpy as jnp
from jax import lax
from jax.experimental import pallas as pl
from jax.experimental.pallas import tpu as pltpu
from jax.sharding import Mesh
from jax.sharding import PartitionSpec as P

ITERS = 3
STEP = 0.8
DIRS = 8
COMPS = 8
VALS = DIRS * COMPS
LANES = 128
RUN = LANES // DIRS
NEAR = ("x", "z0", "core")
FAR = ("z1", "y")


def cmul(left, right):
    return (left[0] * right[0] - left[1] * right[1], left[0] * right[1] + left[1] * right[0])


def cadd(left, right):
    return (left[0] + right[0], left[1] + right[1])


def adjoint(matrix):
    return [(entry[0], -entry[1]) for entry in (matrix[0], matrix[2], matrix[1], matrix[3])]


def product(left, right):
    result = []
    for row in range(2):
        for col in range(2):
            result.append(
                cadd(cmul(left[2 * row], right[col]), cmul(left[2 * row + 1], right[2 + col]))
            )
    return result


def norm_sq(matrix):
    return sum(entry[0] * entry[0] + entry[1] * entry[1] for entry in matrix)


def halves(value):
    high = value.astype(jnp.bfloat16)
    low = (value - high.astype(jnp.float32)).astype(jnp.bfloat16)
    return high, low


def select_sum(left, right, dims):
    rows = left.shape[0]
    both = lax.dot_general(
        jnp.concatenate(halves(left), axis=0), right, (dims, ((), ())),
        preferred_element_type=jnp.float32,
    )
    return both[:rows] + both[rows:]


def pick_sum(left, right, dims):
    rows = right.shape[0]
    both = lax.dot_general(
        left, jnp.concatenate(halves(right), axis=0), (dims, ((), ())),
        preferred_element_type=jnp.float32,
    )
    return both[:, :rows] + both[:, rows:]


def placed(station):
    kept = station & 0b110001111
    return kept | ((station & 0b110000) << 1) | ((station >> 2) & 0b10000)


def open_kernel(*refs):
    sources, (copies_ref, rows_ref), targets, sems = refs[:5], refs[5:7], refs[7:12], refs[12]
    moves = [
        pltpu.make_async_copy(source, target, sems.at[index])
        for index, (source, target) in enumerate(zip(sources, targets))
    ]
    for move in moves:
        move.start()
    for move in moves:
        move.wait()
    gains_ref, weight_ref, live_ref, first_ref, second_ref = targets
    owned = gains_ref.shape[1]
    target = lax.broadcasted_iota(jnp.int32, (owned // 2, owned), 0)
    source = lax.broadcasted_iota(jnp.int32, (owned // 2, owned), 1)
    mine = jnp.concatenate(
        [
            lax.dot_general(
                jnp.where(source == 2 * target + odd, 1.0, 0.0),
                gains_ref[...],
                (((1,), (1,)), ((), ())),
                precision=lax.Precision.HIGHEST,
                preferred_element_type=jnp.float32,
            )
            for odd in range(2)
        ],
        axis=1,
    )
    for at in range(0, copies_ref.shape[0], owned // 2):
        copies_ref[at : at + owned // 2, :] = mine
    live = live_ref[...].astype(jnp.float32)
    lines = [weight_ref[c : c + 1, :] * live for c in range(weight_ref.shape[0])]
    lines += [first_ref[...].astype(jnp.float32), second_ref[...].astype(jnp.float32)]
    cuts = live.shape[1] // LANES
    rows_ref[...] = jnp.concatenate(
        [line[:, cut * LANES : (cut + 1) * LANES] for line in lines for cut in range(cuts)], axis=0
    )


def opened(peers, *args):
    gains, weights = args[:2]
    channels, base = weights.shape
    return pl.pallas_call(
        open_kernel,
        out_shape=(
            jax.ShapeDtypeStruct((peers * gains.shape[1] // 2, LANES), jnp.float32),
            jax.ShapeDtypeStruct(((channels + 2) * base // LANES, LANES), jnp.float32),
        ),
        in_specs=[pl.BlockSpec(memory_space=pltpu.HBM)] * 5,
        out_specs=(pl.BlockSpec(memory_space=pltpu.VMEM),) * 2,
        scratch_shapes=[pltpu.VMEM(a.shape, a.dtype) for a in args]
        + [pltpu.SemaphoreType.DMA((5,))],
        compiler_params=pltpu.CompilerParams(vmem_limit_bytes=16 * 2**20),
        name="opened",
    )(*(pltpu.with_memory_space_constraint(a, pltpu.HBM) for a in args))


def partials_kernel(
    gains_ref, model_ref, vis_ref, rows_ref, out_ref, picked_ref, model_f_ref, terms_ref
):
    pairs = gains_ref.shape[0]
    channels, _, base = model_ref.shape
    cuts = base // LANES
    ends = [rows_ref[channels * cuts + i : channels * cuts + i + 1, :] for i in range(2 * cuts)]
    station = placed(jnp.concatenate(ends, axis=1).astype(jnp.int32))
    rows = lax.broadcasted_iota(jnp.int32, (pairs, 2 * base), 0)
    hot = jnp.where(rows == station // 2, 1.0, 0.0).astype(jnp.bfloat16)
    odd = station % 2 == 1

    both = select_sum(gains_ref[...].T, hot, ((1,), (0,)))
    picked = jnp.where(odd, both[VALS:], both[:VALS])
    for cut in range(2 * cuts):
        picked_ref[cut] = picked[:, cut * LANES : (cut + 1) * LANES]

    def entries(ref, at):
        comps = [ref[at, pl.ds(c, DIRS, stride=COMPS), :] for c in range(COMPS)]
        return [(comps[i], comps[i + 4]) for i in range(4)]

    curvs = [None] * (2 * cuts)
    for cut in range(cuts):
        lanes = slice(cut * LANES, (cut + 1) * LANES)
        near = entries(picked_ref, cut)
        far = entries(picked_ref, cuts + cut)
        totals = None
        for channel in range(channels):
            model_f_ref[0] = model_ref[channel, :, lanes].astype(jnp.float32)
            model = entries(model_f_ref, 0)
            part = channel * cuts + cut
            scale = rows_ref[part : part + 1, :]
            right_a = product(model, adjoint(far))
            left_b = product(near, model)
            each = product(near, right_a)
            vis = vis_ref[channel, :, lanes]
            resid = []
            for index in range(4):
                pred_re = jnp.sum(each[index][0], axis=0, keepdims=True)
                pred_im = jnp.sum(each[index][1], axis=0, keepdims=True)
                resid.append(
                    (
                        scale * (vis[index : index + 1] - pred_re),
                        scale * (vis[index + 4 : index + 5] - pred_im),
                    )
                )
            new = (
                product(resid, adjoint(right_a)),
                product(adjoint(resid), left_b),
                scale * norm_sq(right_a),
                scale * norm_sq(left_b),
            )
            totals = new if totals is None else jax.tree.map(lambda a, b: a + b, totals, new)
        for side in range(2):
            at = side * cuts + cut
            for index, (real, imag) in enumerate(totals[side]):
                terms_ref[at, pl.ds(index, DIRS, stride=COMPS), :] = -real
                terms_ref[at, pl.ds(index + 4, DIRS, stride=COMPS), :] = -imag
            curvs[at] = totals[2 + side]

    terms = jnp.concatenate([terms_ref[at] for at in range(2 * cuts)], axis=1)
    curv = jnp.concatenate(curvs, axis=1)
    spread = jnp.concatenate([jnp.where(odd, 0.0, terms), jnp.where(odd, terms, 0.0)], axis=0)
    grads = pick_sum(hot, spread, ((1,), (1,)))
    wide = jnp.concatenate([curv] * RUN, axis=0)
    seat = lax.broadcasted_iota(jnp.int32, wide.shape, 0) // DIRS
    spread = jnp.where(seat == station % RUN, wide, 0.0)
    rows = lax.broadcasted_iota(jnp.int32, (2 * pairs // RUN, 2 * base), 0)
    hot = jnp.where(rows == station // RUN, 1.0, 0.0).astype(jnp.bfloat16)
    curvs = pick_sum(hot, spread, ((1,), (1,)))
    for peer in range(pairs // RUN):
        at = peer * (RUN + 2)
        out_ref[at : at + RUN, :] = grads[peer * RUN : (peer + 1) * RUN]
        out_ref[at + RUN : at + RUN + 2, :] = curvs[2 * peer : 2 * peer + 2]


def partials(gains, model, vis, rows):
    pairs = gains.shape[0]
    base = model.shape[2]
    return pl.pallas_call(
        partials_kernel,
        out_shape=jax.ShapeDtypeStruct((pairs // RUN * (RUN + 2), LANES), jnp.float32),
        in_specs=[pl.BlockSpec(memory_space=pltpu.VMEM)] * 4,
        out_specs=pl.BlockSpec(memory_space=pltpu.VMEM),
        scratch_shapes=[
            pltpu.VMEM((2 * base // LANES, VALS, LANES), jnp.float32),
            pltpu.VMEM((1, VALS, LANES), jnp.float32),
            pltpu.VMEM((2 * base // LANES, VALS, LANES), jnp.float32),
        ],
        compiler_params=pltpu.CompilerParams(vmem_limit_bytes=16 * 2**20),
        name="partials",
    )(gains, model, vis, rows)


def peers_sum(parts_ref, rows):
    total = parts_ref[0:rows, :]
    for at in range(rows, parts_ref.shape[0], rows):
        total = total + parts_ref[at : at + rows, :]
    return total


def total_kernel(parts_ref, copies_ref):
    total = peers_sum(parts_ref, RUN + 2)
    for at in range(0, copies_ref.shape[0], RUN + 2):
        copies_ref[at : at + RUN + 2, :] = total


def total_halves_kernel(parts_ref, copies_ref):
    total = peers_sum(parts_ref, RUN + 2)
    run = RUN // 2
    count = copies_ref.shape[0] // 2
    for half in range(2):
        own = jnp.concatenate(
            [total[half * run : (half + 1) * run], total[RUN + half : RUN + half + 1]], axis=0
        )
        for at in range(half * count, (half + 1) * count, run + 1):
            copies_ref[at : at + run + 1, :] = own


def total(parts, peers, kernel, rows):
    return pl.pallas_call(
        kernel,
        out_shape=jax.ShapeDtypeStruct((peers * rows, LANES), jnp.float32),
        in_specs=[pl.BlockSpec(memory_space=pltpu.VMEM)],
        out_specs=pl.BlockSpec(memory_space=pltpu.VMEM),
        compiler_params=pltpu.CompilerParams(vmem_limit_bytes=16 * 2**20),
        name="total",
    )(parts)


def stepped(run, at, parts_ref, gains_ref):
    sums = peers_sum(parts_ref, run // 8 * 9)
    grad = sums[:run]
    row = lax.broadcasted_iota(jnp.int32, (run, LANES), 0)
    lane = lax.broadcasted_iota(jnp.int32, (run, LANES), 1)
    curv = sums[run : run + 1]
    if run > 8:
        curv = jnp.where(row < 8, curv, sums[run + 1 : run + 2])
    curv = jnp.where(lane // (2 * DIRS) == row % 8, curv, 0.0)
    source = lax.broadcasted_iota(jnp.int32, (LANES, LANES), 0)
    target = lax.broadcasted_iota(jnp.int32, (LANES, LANES), 1)
    wide = jnp.where(source % (2 * DIRS) == target // COMPS, 1.0, 0.0)
    denom = 1.0 + jnp.dot(
        curv, wide, precision=lax.Precision.HIGHEST, preferred_element_type=jnp.float32
    )
    old = gains_ref[pl.ds(pl.multiple_of(at, run), run), :]
    return old - STEP * grad / denom, grad / jnp.sqrt(denom)


def step_kernel(parts_ref, gains_ref, copies_ref):
    gains, _ = stepped(RUN, lax.axis_index(NEAR) * RUN, parts_ref, gains_ref)
    for at in range(0, copies_ref.shape[0], RUN):
        copies_ref[at : at + RUN, :] = gains


def last_kernel(parts_ref, gains_ref, gains_hbm, white_hbm, gains_out_ref, white_ref, sems):
    owned = gains_out_ref.shape[1]
    run = RUN // 2
    at = lax.axis_index(NEAR) * RUN + lax.axis_index("z1") * run
    source = lax.broadcasted_iota(jnp.int32, (run, owned), 0)
    target = lax.broadcasted_iota(jnp.int32, (run, owned), 1)
    results = stepped(run, at, parts_ref, gains_ref)
    moves = [
        pltpu.make_async_copy(gains_out_ref, gains_hbm, sems.at[0]),
        pltpu.make_async_copy(white_ref, white_hbm, sems.at[1]),
    ]
    for value, out_ref, move in zip(results, (gains_out_ref, white_ref), moves):
        out = None
        for odd in range(2):
            part = lax.dot_general(
                value[:, odd * VALS : (odd + 1) * VALS],
                jnp.where(target == 2 * source + odd, 1.0, 0.0),
                (((0,), (0,)), ((), ())),
                precision=lax.Precision.HIGHEST,
                preferred_element_type=jnp.float32,
            )
            out = part if out is None else out + part
        out_ref[...] = out
        move.start()
    for move in moves:
        move.wait()


def step(parts, gains, peers):
    return pl.pallas_call(
        step_kernel,
        out_shape=jax.ShapeDtypeStruct((peers * RUN, LANES), jnp.float32),
        in_specs=[pl.BlockSpec(memory_space=pltpu.VMEM)] * 2,
        out_specs=pl.BlockSpec(memory_space=pltpu.VMEM),
        compiler_params=pltpu.CompilerParams(vmem_limit_bytes=16 * 2**20),
        name="step",
    )(parts, gains)


def last(parts, gains, owned):
    return pl.pallas_call(
        last_kernel,
        out_shape=(jax.ShapeDtypeStruct((VALS, owned), jnp.float32),) * 2,
        in_specs=[pl.BlockSpec(memory_space=pltpu.VMEM)] * 2,
        out_specs=(pl.BlockSpec(memory_space=pltpu.HBM),) * 2,
        scratch_shapes=[pltpu.VMEM((VALS, owned), jnp.float32)] * 2
        + [pltpu.SemaphoreType.DMA((2,))],
        compiler_params=pltpu.CompilerParams(vmem_limit_bytes=16 * 2**20),
        name="last",
    )(parts, gains)


def exchange(rows, axes, peers):
    count = rows.shape[0]
    sent = rows.reshape(peers, 1, count // peers * LANES)
    return lax.all_to_all(sent, axes, 0, 0).reshape(count, LANES)


def per_device(model, vis, weights, antenna1, antenna2, live, gains):
    base = antenna1.shape[0]
    channels = model.shape[1]
    owned = gains.shape[3]
    model = model.reshape(channels, VALS, base)
    vis, weights = vis[0], weights[0]
    first, second, live = (a.reshape(1, base) for a in (antenna1, antenna2, live))
    copies, rows = opened(32, gains.reshape(VALS, owned), weights, live, first, second)
    full = exchange(copies, NEAR + ("z1",), 32)
    for turn in range(ITERS):
        sent = partials(full, model, vis, rows)
        parts = exchange(sent, NEAR, 16)
        if turn < ITERS - 1:
            sums = exchange(total(parts, 16, total_kernel, RUN + 2), FAR, 16)
            full = exchange(step(sums, full, 16), NEAR, 16)
        else:
            sums = exchange(total(parts, 16, total_halves_kernel, RUN // 2 + 1), FAR, 16)
    return tuple(out.reshape(gains.shape) for out in last(sums, full, owned))


def solution(mesh):
    fine = Mesh(mesh.devices.reshape(8, 4, 2, 2, 2, 2), ("y", "x", "z1", "z0", "core", "chan"))
    bl = ("x", "z1", "z0", "core")
    return jax.shard_map(
        per_device,
        mesh=fine,
        in_specs=(
            P("y", "chan", None, None, bl),
            P("y", "chan", None, bl),
            P("y", "chan", bl),
            P(bl),
            P(bl),
            P(bl),
            P("chan", None, None, bl),
        ),
        out_specs=(P("chan", None, None, bl), P("chan", None, None, bl)),
        check_vma=False,
    )
```
